256 devices in a mesh: row: 8 (over z), col: 32 (over y, x, core).
Axes of the slice: x: 4, y: 4, z: 8, core: 2. Of those that a mesh axis runs over, the one named last changes fastest.
Arguments:
- src_points: float32 [64, 32768], P(None, ('row', 'col')), may hold values from -3 to 3
- tgt_points: float32 [64, 32768], P(None, ('col', 'row')), may hold values from -0.75 to 0.75
- src_logmass: float32 [32768], P('row'), may hold values from -1 to 1
- tgt_logmass: float32 [32768], P('col'), may hold values from -1 to 1
Outputs:
- src_potential: float32 [32768], P('row')
- tgt_potential: float32 [32768], P('col')
The draws below stay inside these ranges and needn't reach their ends.
All inputs are finite; a program needn't handle non-finite values.
Results may differ from the reference program's by a relative error of at most 0.00018.
Values sent between devices are 32-bit elements; how exact they have to be, the bound alone decides.
A program may use at most 64 MiB of HBM per device.

```python
import jax
import jax.numpy as jnp
from jax import lax

D = 64
ITERS = 2
NS = 32768
NT = 32768


def draw_src_points(key, part):
    key = jax.random.fold_in(key, 7)
    first = jax.random.fold_in(key, 0)
    base = jax.random.normal(first, (D, NS), jnp.float32) * 0.125
    return jnp.clip(base, -0.75, 0.75)


def draw_tgt_points(key, part):
    key = jax.random.fold_in(key, 11)
    first, second = jax.random.split(key)
    base = jax.random.normal(first, (D, NT), jnp.float32) * 0.125
    index = jnp.arange(NT, dtype=jnp.int32)
    extra = jax.random.randint(second, (NT,), 0, 32) == 0
    moved = jnp.logical_or(index < NT // 8, extra)
    offset = jnp.where(moved, 0.4, 0.0).astype(jnp.float32)
    return jnp.clip(base + offset[None, :], -0.75, 0.75)


def block_levels(stream_key, dims, cuts, least, top_value):
    level = 1.0
    for position, parts in cuts:
        heights = jax.random.uniform(jax.random.fold_in(jax.random.fold_in(stream_key, 6), position), (parts,), jnp.float32, least / len(cuts), top_value / len(cuts))
        level = level * jnp.repeat(jnp.exp(heights), dims[position] // parts).reshape((-1,) + (1,) * (len(dims) - 1 - position))
    return level


def setup_inputs(seed: int = 0) -> dict:
    key_of = jax.random.split(jax.random.key(seed), 5)
    src_points = draw_src_points(jax.random.fold_in(key_of[4], 71), 0)
    tgt_points = draw_tgt_points(jax.random.fold_in(key_of[4], 71), 0)
    src_logmass = jnp.clip(jax.random.uniform(key_of[2], (NS,), jnp.float32, -1.0, 1.0) * block_levels(key_of[2], (NS,), ((0, 8),), -0.4, 0.0), -1.0, 1.0)
    tgt_logmass = jnp.clip(jax.random.uniform(key_of[3], (NT,), jnp.float32, -1.0, 1.0) * block_levels(key_of[3], (NT,), ((0, 32),), -0.4, 0.0), -1.0, 1.0)
    return {"src_points": src_points, "tgt_points": tgt_points, "src_logmass": src_logmass, "tgt_logmass": tgt_logmass}


EPSILON = 0.05


def tile_costs(xb, xnb, yb, ynb):
    cross = lax.dot_general(xb, yb, (((0,), (0,)), ((), ())), precision=lax.Precision.HIGHEST, preferred_element_type=jnp.float32)
    return xnb[:, None] + ynb[None, :] - 2.0 * cross


def reference(src_points, tgt_points, src_logmass, tgt_logmass):
    src_norm = jnp.sum(src_points * src_points, axis=0)
    tgt_norm = jnp.sum(tgt_points * tgt_points, axis=0)
    sblk = min(512, NS)
    tblk = min(512, NT)
    src_blocks = src_points.reshape(D, NS // sblk, sblk).transpose(1, 0, 2)
    src_nblocks = src_norm.reshape(NS // sblk, sblk)
    tgt_blocks = tgt_points.reshape(D, NT // tblk, tblk).transpose(1, 0, 2)
    tgt_nblocks = tgt_norm.reshape(NT // tblk, tblk)
    tgt_pot = jnp.zeros((NT,), jnp.float32)
    src_pot = jnp.zeros((NS,), jnp.float32)
    for step in range(ITERS):
        def source_rows(args):
            xb, xnb = args
            scores = (tgt_pot[None, :] - tile_costs(xb, xnb, tgt_points, tgt_norm)) / EPSILON + tgt_logmass[None, :]
            top = jnp.max(scores, axis=1)
            return -EPSILON * (top + jnp.log(jnp.sum(jnp.exp(scores - top[:, None]), axis=1)))

        src_pot = lax.map(source_rows, (src_blocks, src_nblocks)).reshape(NS)

        def target_cols(args):
            yb, ynb = args
            scores = (src_pot[:, None] - tile_costs(src_points, src_norm, yb, ynb)) / EPSILON + src_logmass[:, None]
            top = jnp.max(scores, axis=0)
            return -EPSILON * (top + jnp.log(jnp.sum(jnp.exp(scores - top[None, :]), axis=0)))

        tgt_pot = lax.map(target_cols, (tgt_blocks, tgt_nblocks)).reshape(NT)
    return src_pot, tgt_pot
```

```python
import functools
import math

import jax
import jax.numpy as jnp
from jax import lax
from jax.experimental import pallas as pl
from jax.experimental.pallas import tpu as pltpu
from jax.sharding import PartitionSpec as P

MESH = pl.DeviceIdType.MESH
EPSILON = 0.05
LOG2E = math.log2(math.e)
SCORE = LOG2E / EPSILON
UNIT = EPSILON / LOG2E
D = 64
B = 128
NB = 16
N = NB * B
F32 = jnp.float32
BF16 = jnp.bfloat16

PLANE = sorted(
    [(dy, dx) for dy in range(4) for dx in range(4) if (dy, dx) != (0, 0)],
    key=lambda o: min(o[0], 4 - o[0]) + min(o[1], 4 - o[1]),
)
RING = sorted(range(1, 8), key=lambda d: min(d, 8 - d))
COLUMN = sorted(
    [(dz, dc) for dz in range(8) for dc in range(2) if (dz, dc) != (0, 0)],
    key=lambda o: min(o[0], 8 - o[0]),
)


def lse_rows(values):
    top = jnp.max(values, axis=0)
    return top + jnp.log(jnp.sum(jnp.exp2(values - top[None]), axis=0)) * LOG2E


def kernel(
    x_ref, y_ref, a_ref, b_ref, f_ref, g_ref,
    xs, ys, bfull, X, Y, T, xn, yn, gb, fa, fb8, mbuf, sbuf, R8, v8,
    ex1, ex2, ex3, ex4, fsib,
    x_send, x_recv, y_send, y_recv, p_send, p_recv, b_sem, e_send, e_recv, f_sem,
):
    z = lax.axis_index("row")
    c = lax.axis_index("col")
    core = lax.rem(c, 2)
    chip = lax.div(c, 2)
    xi = lax.rem(chip, 4)
    yi = lax.div(chip, 4)
    here = core * 8 + z

    def plane(o):
        dy, dx = o
        return (z, (lax.rem(yi + dy, 4) * 4 + lax.rem(xi + dx, 4)) * 2 + core)

    def column(o):
        dz, dc = o
        return (lax.rem(z + dz, 8), chip * 2 + lax.rem(core + dc, 2))

    sibling = column((0, 1))

    def send(src, dst, ssem, rsem, dev):
        copy = pltpu.make_async_remote_copy(
            src_ref=src, dst_ref=dst, send_sem=ssem, recv_sem=rsem, device_id=dev, device_id_type=MESH
        )
        copy.start()

    def wait(ref, sem):
        pltpu.make_async_copy(ref, ref, sem).wait()

    barrier = pltpu.get_barrier_semaphore()
    for o in PLANE:
        pl.semaphore_signal(barrier, inc=1, device_id=plane(o), device_id_type=MESH)
    for o in COLUMN:
        pl.semaphore_signal(barrier, inc=1, device_id=column(o), device_id_type=MESH)
    xs[chip] = x_ref[...]
    ys[here] = y_ref[...]
    mine8 = pl.ds(pl.multiple_of(core * 8, 8), 8)
    bfull[mine8, :] = b_ref[...]
    pl.semaphore_wait(barrier, len(PLANE) + len(COLUMN))

    for k, dz in enumerate(RING):
        send(ys.at[here], ys.at[here], y_send, y_recv.at[k], column((dz, 0)))
    send(ys.at[here], ys.at[here], p_send, p_recv.at[7], sibling)
    send(bfull.at[mine8], bfull.at[mine8], b_sem.at[0], b_sem.at[1], sibling)
    for k, o in enumerate(PLANE):
        send(xs.at[chip], xs.at[chip], x_send, x_recv.at[k], plane(o))
    for k, dz in enumerate(RING):
        slot = core * 8 + lax.rem(z + 8 - dz, 8)
        wait(ys.at[slot], y_recv.at[k])
        send(ys.at[slot], ys.at[slot], p_send, p_recv.at[k], sibling)
    for k, o in enumerate(PLANE):
        wait(xs.at[0], x_recv.at[k])

    ones = (lax.broadcasted_iota(jnp.int32, (D, B), 0) < 3).astype(BF16)

    def build_source(m, _):
        x = xs[m]
        xn[pl.ds(m, 1), :] = jnp.sum(x * x, axis=0, keepdims=True)
        scaled = x * (2.0 * SCORE)
        hi = scaled.astype(BF16)
        lo = (scaled - hi.astype(F32)).astype(BF16)
        at = pl.ds(pl.multiple_of(m * B, B), B)
        X[0:64, at] = hi
        X[64:128, at] = ones
        X[128:192, at] = hi
        X[192:256, at] = lo
        return 0

    lax.fori_loop(0, NB, build_source, 0)

    for k in range(8):
        wait(ys.at[0], p_recv.at[k])
    wait(bfull.at[mine8], b_sem.at[1])

    left = lax.broadcasted_iota(jnp.int32, (B, B), 1) < D

    def build_target(t, _):
        y = ys[t]
        norm = jnp.sum(y * y, axis=0, keepdims=True)
        yn[pl.ds(t, 1), :] = norm
        bias = bfull[pl.ds(t, 1), :] * LOG2E - norm * SCORE
        gb[pl.ds(t, 1), :] = bias
        hi = bias.astype(BF16).astype(F32)
        mid = (bias - hi).astype(BF16).astype(F32)
        lo = bias - hi - mid
        row = lax.broadcasted_iota(jnp.int32, (D, B), 0)
        tail = jnp.where(row == 0, hi, jnp.where(row == 1, mid, jnp.where(row == 2, lo, 0.0)))
        both = jnp.concatenate([y, tail], axis=0).T
        top = both.astype(BF16).astype(F32)
        rest = jnp.where(left, both - top, pltpu.roll(top, D, 1))
        at = pl.ds(pl.multiple_of(t * B, B), B)
        Y[at, 0:128] = top.astype(BF16)
        Y[at, 128:256] = rest.astype(BF16)
        return 0

    lax.fori_loop(0, NB, build_target, 0)

    def half1(n, _):
        at = pl.ds(pl.multiple_of(n * 256, 256), 256)
        T[:, at] = jnp.dot(Y[...], X[:, at], preferred_element_type=F32)
        for u in range(2):
            lane = pl.ds(pl.multiple_of(n * 256 + u * B, B), B)

            def strip(q, carry):
                m, s = carry
                rows = T[pl.ds(pl.multiple_of(q * 128, 128), 128), lane].reshape(16, 8, B)
                new = jnp.maximum(m, jnp.max(rows, axis=0))
                s = s * jnp.exp2(m - new) + jnp.sum(jnp.exp2(rows - new[None]), axis=0)
                return new, s

            m, s = lax.fori_loop(
                0, NB, strip, (jnp.full((8, B), -1e30, F32), jnp.zeros((8, B), F32))
            )
            top = jnp.max(m, axis=0, keepdims=True)
            total = jnp.sum(s * jnp.exp2(m - top), axis=0, keepdims=True)
            ex1[chip, pl.ds(n * 2 + u, 1), :] = top + jnp.log(total) * LOG2E
        return 0

    lax.fori_loop(0, 8, half1, 0)

    def exchange(ex, mine, targets, e):
        for o in reversed(targets):
            send(ex.at[mine], ex.at[mine], e_send.at[e], e_recv.at[e], o)
        wait(ex.at[pl.ds(0, 15)], e_recv.at[e])

    planes = [plane(o) for o in PLANE]
    columns = [column(o) for o in COLUMN]

    exchange(ex1, chip, planes, 0)
    a2 = a_ref[pl.ds(core, NB, stride=2), :] * LOG2E
    first = a2 - lse_rows(ex1[...])
    fa[...] = first
    for n in range(NB):
        fb8[:, n * B : (n + 1) * B] = jnp.broadcast_to(fa[n : n + 1, :], (8, B))

    def half2(t, _):
        def strip(q, _):
            at = pl.ds(pl.multiple_of(t * B + q * 8, 8), 8)
            parts = []
            for n in range(NB):
                lane = slice(n * B, (n + 1) * B)
                value = T[at, lane] + fb8[:, lane]
                T[at, lane] = value
                parts.append(value)
            tops = parts
            while len(tops) > 1:
                tops = [jnp.maximum(p, q) for p, q in zip(tops[::2], tops[1::2])]
            sums = [jnp.exp2(p - tops[0]) for p in parts]
            while len(sums) > 1:
                sums = [p + q for p, q in zip(sums[::2], sums[1::2])]
            at = pl.ds(pl.multiple_of(q * 8, 8), 8)
            mbuf[at, :] = tops[0]
            sbuf[at, :] = sums[0]
            return 0

        lax.fori_loop(0, NB, strip, 0)
        m = mbuf[...].T
        s = sbuf[...].T
        top = jnp.max(m, axis=0, keepdims=True)
        total = jnp.sum(s * jnp.exp2(m - top), axis=0, keepdims=True)
        ex2[here, pl.ds(t, 1), :] = top + jnp.log(total) * LOG2E
        return 0

    lax.fori_loop(0, NB, half2, 0)
    exchange(ex2, here, columns, 1)
    b2 = bfull[...] * LOG2E
    total2 = lse_rows(ex2[...])
    gb[...] = gb[...] - total2 + b2
    fa[...] = b2 - total2

    R8[...] = jnp.zeros((8, N), F32)

    def half3(t, _):
        mbuf[...] = jnp.broadcast_to(fa[pl.ds(t, 1), :], (B, B)).T

        def strip(q, _):
            at = pl.ds(pl.multiple_of(t * B + q * 8, 8), 8)
            shift = mbuf[pl.ds(pl.multiple_of(q * 8, 8), 8), :]
            for n in range(NB):
                lane = slice(n * B, (n + 1) * B)
                value = jnp.exp2(T[at, lane] + shift)
                T[at, lane] = value
                R8[:, lane] = R8[:, lane] + value
            return 0

        lax.fori_loop(0, NB, strip, 0)
        return 0

    lax.fori_loop(0, NB, half3, 0)
    for n in range(NB):
        ex3[chip, n : n + 1, :] = jnp.sum(R8[:, n * B : (n + 1) * B], axis=0, keepdims=True)
    exchange(ex3, chip, planes, 2)
    total3 = jnp.sum(ex3[...], axis=0)
    second = first - jnp.log(total3) * LOG2E
    fsib[0] = xn[...] + second * UNIT
    send(fsib.at[0], fsib.at[1], f_sem.at[0], f_sem.at[1], sibling)
    fa[...] = jnp.exp2(a2) / total3
    for n in range(NB):
        v8[:, n * B : (n + 1) * B] = jnp.broadcast_to(fa[n : n + 1, :], (8, B))

    def half4(t, _):
        def strip(q, _):
            at = pl.ds(pl.multiple_of(t * B + q * 8, 8), 8)
            sums = []
            for n in range(NB):
                lane = slice(n * B, (n + 1) * B)
                sums.append(T[at, lane] * v8[:, lane])
            while len(sums) > 1:
                sums = [p + q for p, q in zip(sums[::2], sums[1::2])]
            sbuf[pl.ds(pl.multiple_of(q * 8, 8), 8), :] = sums[0]
            return 0

        lax.fori_loop(0, NB, strip, 0)
        ex4[here, pl.ds(t, 1), :] = jnp.sum(sbuf[...].T, axis=0, keepdims=True)
        return 0

    lax.fori_loop(0, NB, half4, 0)
    exchange(ex4, here, columns, 3)
    total4 = jnp.sum(ex4[...], axis=0)
    fa[...] = yn[...] + (gb[...] - jnp.log(total4) * LOG2E) * UNIT
    g_ref[...] = fa[mine8, :]
    wait(fsib.at[1], f_sem.at[1])
    f_ref[pl.ds(core, NB, stride=2), :] = fsib[0]
    f_ref[pl.ds(1 - core, NB, stride=2), :] = fsib[1]

    wait(xs.at[pl.ds(0, 15)], x_send)
    wait(ys.at[pl.ds(0, 7)], y_send)
    wait(ys.at[pl.ds(0, 8)], p_send)
    wait(bfull.at[mine8], b_sem.at[0])
    wait(fsib.at[0], f_sem.at[0])
    for e, ex in enumerate((ex1, ex2, ex3, ex4)):
        wait(ex.at[pl.ds(0, 15)], e_send.at[e])


def on_device(src_points, tgt_points, src_logmass, tgt_logmass):
    vmem = pl.BlockSpec(memory_space=pltpu.VMEM)
    dma = pltpu.SemaphoreType.DMA
    exchange = pltpu.VMEM((NB, NB, B), F32)
    f, g = pl.pallas_call(
        kernel,
        out_shape=(jax.ShapeDtypeStruct((32, B), F32), jax.ShapeDtypeStruct((8, B), F32)),
        in_specs=[vmem] * 4,
        out_specs=(vmem, vmem),
        scratch_shapes=[
            pltpu.VMEM((NB, D, B), F32),
            pltpu.VMEM((NB, D, B), F32),
            pltpu.VMEM((NB, B), F32),
            pltpu.VMEM((256, N), BF16),
            pltpu.VMEM((N, 256), BF16),
            pltpu.VMEM((N, N), F32),
            pltpu.VMEM((NB, B), F32),
            pltpu.VMEM((NB, B), F32),
            pltpu.VMEM((NB, B), F32),
            pltpu.VMEM((NB, B), F32),
            pltpu.VMEM((8, N), F32),
            pltpu.VMEM((B, B), F32),
            pltpu.VMEM((B, B), F32),
            pltpu.VMEM((8, N), F32),
            pltpu.VMEM((8, N), F32),
            exchange, exchange, exchange, exchange,
            pltpu.VMEM((2, NB, B), F32),
            dma, dma((15,)), dma, dma((7,)), dma, dma((8,)), dma((2,)), dma((4,)), dma((4,)), dma((2,)),
        ],
        compiler_params=pltpu.CompilerParams(
            collective_id=0, has_side_effects=True, vmem_limit_bytes=56 << 20
        ),
    )(src_points, tgt_points, src_logmass.reshape(32, B), tgt_logmass.reshape(8, B))
    return f.reshape(-1), g.reshape(-1)


def solution(mesh):
    return jax.shard_map(
        on_device,
        mesh=mesh,
        in_specs=(P(None, ("row", "col")), P(None, ("col", "row")), P("row"), P("col")),
        out_specs=(P("row"), P("col")),
        check_vma=False,
    )
```

```python
import functools
import math

import jax
import jax.numpy as jnp
from jax import lax
from jax.experimental import pallas as pl
from jax.experimental.pallas import tpu as pltpu
from jax.sharding import PartitionSpec as P

MESH = pl.DeviceIdType.MESH
EPSILON = 0.05
LOG2E = math.log2(math.e)
SCORE = LOG2E / EPSILON
UNIT = EPSILON / LOG2E
D = 64
B = 128
NB = 16
N = NB * B
F32 = jnp.float32
BF16 = jnp.bfloat16

PLANE = sorted(
    [(dy, dx) for dy in range(4) for dx in range(4) if (dy, dx) != (0, 0)],
    key=lambda o: min(o[0], 4 - o[0]) + min(o[1], 4 - o[1]),
)
RING = sorted(range(1, 8), key=lambda d: min(d, 8 - d))
COLUMN = sorted(
    [(dz, dc) for dz in range(8) for dc in range(2) if (dz, dc) != (0, 0)],
    key=lambda o: min(o[0], 8 - o[0]),
)


def lse_rows(values):
    top = jnp.max(values, axis=0)
    return top + jnp.log(jnp.sum(jnp.exp2(values - top[None]), axis=0)) * LOG2E


def tree(op, parts):
    while len(parts) > 1:
        parts = [op(p, q) for p, q in zip(parts[::2], parts[1::2])]
    return parts[0]


def kernel(
    x_ref, y_ref, a_ref, b_ref, f_ref, g_ref,
    xs, ys, bfull, X, Y, T, xn, yn, gb, fa, fb8, mbuf, sbuf, R8, v8,
    ex1, ex2, ex3, ex4, fsib,
    x_send, x_recv, y_send, y_recv, p_send, p_recv, b_sem, e_send, e_recv, f_sem,
):
    z = lax.axis_index("row")
    c = lax.axis_index("col")
    core = lax.rem(c, 2)
    chip = lax.div(c, 2)
    xi = lax.rem(chip, 4)
    yi = lax.div(chip, 4)
    here = core * 8 + z

    def plane(o):
        dy, dx = o
        return (z, (lax.rem(yi + dy, 4) * 4 + lax.rem(xi + dx, 4)) * 2 + core)

    def column(o):
        dz, dc = o
        return (lax.rem(z + dz, 8), chip * 2 + lax.rem(core + dc, 2))

    sibling = column((0, 1))

    def send(src, dst, ssem, rsem, dev):
        copy = pltpu.make_async_remote_copy(
            src_ref=src, dst_ref=dst, send_sem=ssem, recv_sem=rsem, device_id=dev, device_id_type=MESH
        )
        copy.start()

    def wait(ref, sem):
        pltpu.make_async_copy(ref, ref, sem).wait()

    barrier = pltpu.get_barrier_semaphore()
    for o in PLANE:
        pl.semaphore_signal(barrier, inc=1, device_id=plane(o), device_id_type=MESH)
    for o in COLUMN:
        pl.semaphore_signal(barrier, inc=1, device_id=column(o), device_id_type=MESH)
    xs[chip] = x_ref[...]
    ys[here] = y_ref[...]
    mine8 = pl.ds(pl.multiple_of(core * 8, 8), 8)
    bfull[mine8, :] = b_ref[...]
    pl.semaphore_wait(barrier, len(PLANE) + len(COLUMN))

    for k, dz in enumerate(RING):
        send(ys.at[here], ys.at[here], y_send, y_recv.at[k], column((dz, 0)))
    send(ys.at[here], ys.at[here], p_send, p_recv.at[7], sibling)
    send(bfull.at[mine8], bfull.at[mine8], b_sem.at[0], b_sem.at[1], sibling)
    for k, o in enumerate(PLANE):
        send(xs.at[chip], xs.at[chip], x_send, x_recv.at[k], plane(o))
    for k, dz in enumerate(RING):
        slot = core * 8 + lax.rem(z + 8 - dz, 8)
        wait(ys.at[slot], y_recv.at[k])
        send(ys.at[slot], ys.at[slot], p_send, p_recv.at[k], sibling)
    for k, o in enumerate(PLANE):
        wait(xs.at[0], x_recv.at[k])

    ones = (lax.broadcasted_iota(jnp.int32, (D, B), 0) < 3).astype(BF16)

    def build_source(m, _):
        x = xs[m]
        xn[pl.ds(m, 1), :] = jnp.sum(x * x, axis=0, keepdims=True)
        scaled = x * (2.0 * SCORE)
        hi = scaled.astype(BF16)
        lo = (scaled - hi.astype(F32)).astype(BF16)
        at = pl.ds(pl.multiple_of(m * B, B), B)
        X[0:64, at] = hi
        X[64:128, at] = ones
        X[128:192, at] = hi
        X[192:256, at] = lo
        return 0

    lax.fori_loop(0, NB, build_source, 0)

    for k in range(8):
        wait(ys.at[0], p_recv.at[k])
    wait(bfull.at[mine8], b_sem.at[1])

    left = lax.broadcasted_iota(jnp.int32, (B, B), 1) < D

    def build_target(t, _):
        for q in range(4):
            build_one(t * 4 + q)
        return 0

    def build_one(t):
        y = ys[t]
        norm = jnp.sum(y * y, axis=0, keepdims=True)
        yn[pl.ds(t, 1), :] = norm
        bias = bfull[pl.ds(t, 1), :] * LOG2E - norm * SCORE
        gb[pl.ds(t, 1), :] = bias
        hi = bias.astype(BF16).astype(F32)
        mid = (bias - hi).astype(BF16).astype(F32)
        lo = bias - hi - mid
        row = lax.broadcasted_iota(jnp.int32, (D, B), 0)
        tail = jnp.where(row == 0, hi, jnp.where(row == 1, mid, jnp.where(row == 2, lo, 0.0)))
        both = jnp.concatenate([y, tail], axis=0).T
        top = both.astype(BF16).astype(F32)
        rest = jnp.where(left, both - top, pltpu.roll(top, D, 1))
        at = pl.ds(pl.multiple_of(t * B, B), B)
        Y[at, 0:128] = top.astype(BF16)
        Y[at, 128:256] = rest.astype(BF16)

    lax.fori_loop(0, 4, build_target, 0)

    def half1(n, _):
        at = pl.ds(pl.multiple_of(n * 256, 256), 256)
        T[:, at] = jnp.dot(Y[...], X[:, at], preferred_element_type=F32)
        for u in range(2):
            lane = pl.ds(pl.multiple_of(n * 256 + u * B, B), B)
            m = s = None
            for q in range(NB):
                rows = [T[q * B + r * 8 : q * B + r * 8 + 8, lane] for r in range(16)]
                new = tree(jnp.maximum, rows)
                if q:
                    new = jnp.maximum(m, new)
                total = tree(jnp.add, [jnp.exp2(r - new) for r in rows])
                s = total + s * jnp.exp2(m - new) if q else total
                m = new
            top = jnp.max(m, axis=0, keepdims=True)
            total = jnp.sum(s * jnp.exp2(m - top), axis=0, keepdims=True)
            ex1[chip, pl.ds(n * 2 + u, 1), :] = top + jnp.log(total) * LOG2E
        return 0

    lax.fori_loop(0, 8, half1, 0)

    def exchange(ex, mine, targets, e):
        for o in reversed(targets):
            send(ex.at[mine], ex.at[mine], e_send.at[e], e_recv.at[e], o)
        wait(ex.at[pl.ds(0, 15)], e_recv.at[e])

    planes = [plane(o) for o in PLANE]
    columns = [column(o) for o in COLUMN]

    exchange(ex1, chip, planes, 0)
    a2 = a_ref[pl.ds(core, NB, stride=2), :] * LOG2E
    first = a2 - lse_rows(ex1[...])
    fa[...] = first
    for n in range(NB):
        fb8[:, n * B : (n + 1) * B] = jnp.broadcast_to(fa[n : n + 1, :], (8, B))

    def half2(t, _):
        block = pl.ds(pl.multiple_of(t * B, B), B)
        Tb, mb, sb = T.at[block], mbuf.at[block], sbuf.at[block]
        for q in range(NB):
            at = slice(q * 8, q * 8 + 8)
            parts = []
            for n in range(NB):
                lane = slice(n * B, (n + 1) * B)
                value = Tb[at, lane] + fb8[:, lane]
                Tb[at, lane] = value
                parts.append(value)
            top = tree(jnp.maximum, parts)
            mb[at, :] = top
            sb[at, :] = tree(jnp.add, [jnp.exp2(p - top) for p in parts])
        return 0

    lax.fori_loop(0, NB, half2, 0)

    def join2(t, _):
        for q in range(4):
            at = pl.ds(pl.multiple_of(t * 4 * B, B) + q * B, B)
            m = mbuf[at, :].T
            s = sbuf[at, :].T
            top = jnp.max(m, axis=0, keepdims=True)
            total = jnp.sum(s * jnp.exp2(m - top), axis=0, keepdims=True)
            ex2[here, pl.ds(t * 4 + q, 1), :] = top + jnp.log(total) * LOG2E
        return 0

    lax.fori_loop(0, 4, join2, 0)
    exchange(ex2, here, columns, 1)
    b2 = bfull[...] * LOG2E
    total2 = lse_rows(ex2[...])
    gb[...] = gb[...] - total2 + b2
    fa[...] = b2 - total2

    R8[...] = jnp.zeros((8, N), F32)

    def spread(t, _):
        for q in range(4):
            at = pl.ds(pl.multiple_of(t * 4 * B, B) + q * B, B)
            mbuf[at, :] = jnp.broadcast_to(fa[pl.ds(t * 4 + q, 1), :], (B, B)).T
        return 0

    lax.fori_loop(0, 4, spread, 0)

    def half3(t, _):
        block = pl.ds(pl.multiple_of(t * B, B), B)
        Tb, mb = T.at[block], mbuf.at[block]
        for h in range(2):
            ats = [slice((h * 8 + q) * 8, (h * 8 + q) * 8 + 8) for q in range(8)]
            shifts = [mb[at, :] for at in ats]
            for n in range(NB):
                lane = slice(n * B, (n + 1) * B)
                values = []
                for at, shift in zip(ats, shifts):
                    value = jnp.exp2(Tb[at, lane] + shift)
                    Tb[at, lane] = value
                    values.append(value)
                R8[:, lane] = R8[:, lane] + tree(jnp.add, values)
        return 0

    lax.fori_loop(0, NB, half3, 0)
    for n in range(NB):
        ex3[chip, n : n + 1, :] = jnp.sum(R8[:, n * B : (n + 1) * B], axis=0, keepdims=True)
    exchange(ex3, chip, planes, 2)
    total3 = jnp.sum(ex3[...], axis=0)
    second = first - jnp.log(total3) * LOG2E
    fsib[0] = xn[...] + second * UNIT
    send(fsib.at[0], fsib.at[1], f_sem.at[0], f_sem.at[1], sibling)
    fa[...] = jnp.exp2(a2) / total3
    for n in range(NB):
        v8[:, n * B : (n + 1) * B] = jnp.broadcast_to(fa[n : n + 1, :], (8, B))

    def half4(t, _):
        block = pl.ds(pl.multiple_of(t * B, B), B)
        Tb, sb = T.at[block], sbuf.at[block]
        for h in range(2):
            ats = [slice((h * 8 + q) * 8, (h * 8 + q) * 8 + 8) for q in range(8)]
            sums = [None] * 8
            for n in range(NB):
                lane = slice(n * B, (n + 1) * B)
                weight = v8[:, lane]
                for q, at in enumerate(ats):
                    value = Tb[at, lane] * weight
                    sums[q] = value if n == 0 else sums[q] + value
            for q, at in enumerate(ats):
                sb[at, :] = sums[q]
        return 0

    lax.fori_loop(0, NB, half4, 0)

    def join4(t, _):
        for q in range(4):
            at = pl.ds(pl.multiple_of(t * 4 * B, B) + q * B, B)
            ex4[here, pl.ds(t * 4 + q, 1), :] = jnp.sum(sbuf[at, :].T, axis=0, keepdims=True)
        return 0

    lax.fori_loop(0, 4, join4, 0)
    exchange(ex4, here, columns, 3)
    total4 = jnp.sum(ex4[...], axis=0)
    fa[...] = yn[...] + (gb[...] - jnp.log(total4) * LOG2E) * UNIT
    g_ref[...] = fa[mine8, :]
    wait(fsib.at[1], f_sem.at[1])
    f_ref[pl.ds(core, NB, stride=2), :] = fsib[0]
    f_ref[pl.ds(1 - core, NB, stride=2), :] = fsib[1]

    wait(xs.at[pl.ds(0, 15)], x_send)
    wait(ys.at[pl.ds(0, 7)], y_send)
    wait(ys.at[pl.ds(0, 8)], p_send)
    wait(bfull.at[mine8], b_sem.at[0])
    wait(fsib.at[0], f_sem.at[0])
    for e, ex in enumerate((ex1, ex2, ex3, ex4)):
        wait(ex.at[pl.ds(0, 15)], e_send.at[e])


def on_device(src_points, tgt_points, src_logmass, tgt_logmass):
    vmem = pl.BlockSpec(memory_space=pltpu.VMEM)
    dma = pltpu.SemaphoreType.DMA
    exchange = pltpu.VMEM((NB, NB, B), F32)
    f, g = pl.pallas_call(
        kernel,
        out_shape=(jax.ShapeDtypeStruct((32, B), F32), jax.ShapeDtypeStruct((8, B), F32)),
        in_specs=[vmem] * 4,
        out_specs=(vmem, vmem),
        scratch_shapes=[
            pltpu.VMEM((NB, D, B), F32),
            pltpu.VMEM((NB, D, B), F32),
            pltpu.VMEM((NB, B), F32),
            pltpu.VMEM((256, N), BF16),
            pltpu.VMEM((N, 256), BF16),
            pltpu.VMEM((N, N), F32),
            pltpu.VMEM((NB, B), F32),
            pltpu.VMEM((NB, B), F32),
            pltpu.VMEM((NB, B), F32),
            pltpu.VMEM((NB, B), F32),
            pltpu.VMEM((8, N), F32),
            pltpu.VMEM((N, B), F32),
            pltpu.VMEM((N, B), F32),
            pltpu.VMEM((8, N), F32),
            pltpu.VMEM((8, N), F32),
            exchange, exchange, exchange, exchange,
            pltpu.VMEM((2, NB, B), F32),
            dma, dma((15,)), dma, dma((7,)), dma, dma((8,)), dma((2,)), dma((4,)), dma((4,)), dma((2,)),
        ],
        compiler_params=pltpu.CompilerParams(
            collective_id=0, has_side_effects=True, vmem_limit_bytes=56 << 20
        ),
    )(src_points, tgt_points, src_logmass.reshape(32, B), tgt_logmass.reshape(8, B))
    return f.reshape(-1), g.reshape(-1)


def solution(mesh):
    return jax.shard_map(
        on_device,
        mesh=mesh,
        in_specs=(P(None, ("row", "col")), P(None, ("col", "row")), P("row"), P("col")),
        out_specs=(P("row"), P("col")),
        check_vma=False,
    )
```

```python
import functools
import math

import jax
import jax.numpy as jnp
from jax import lax
from jax.experimental import pallas as pl
from jax.experimental.pallas import tpu as pltpu
from jax.sharding import PartitionSpec as P

MESH = pl.DeviceIdType.MESH
EPSILON = 0.05
LOG2E = math.log2(math.e)
SCORE = LOG2E / EPSILON
UNIT = EPSILON / LOG2E
D = 64
B = 128
NB = 16
N = NB * B
F32 = jnp.float32
BF16 = jnp.bfloat16

PLANE = [(dy, dx) for dy in range(4) for dx in range(4) if (dy, dx) != (0, 0)]
RING = [1, 7, 2, 6, 3, 5, 4]
COLUMN = sorted(
    [(dz, dc) for dz in range(8) for dc in range(2) if (dz, dc) != (0, 0)],
    key=lambda o: min(o[0], 8 - o[0]),
)
FAR = sorted(PLANE, key=lambda o: -min(o[0], 4 - o[0]) - min(o[1], 4 - o[1]))


def lse_rows(values):
    top = jnp.max(values, axis=0)
    return top + jnp.log(jnp.sum(jnp.exp2(values - top[None]), axis=0)) * LOG2E


def tree(op, parts):
    while len(parts) > 1:
        parts = [op(p, q) for p, q in zip(parts[::2], parts[1::2])]
    return parts[0]


def kernel(
    x_ref, y_ref, a_ref, b_ref, f_ref, g_ref,
    xs, ys, av, bown, bsib, X, Y, T, MS, xn, yn, gb, ba, fa, fb8, mbuf, sbuf, R8, v8,
    ex1, ex2, ex3, ex4, fsib,
    in_sem, x_send, x_recv, y_send, y_recv, p_send, p_recv, b_sem, e_send, e_recv, f_sem,
):
    z = lax.axis_index("row")
    c = lax.axis_index("col")
    core = lax.rem(c, 2)
    chip = lax.div(c, 2)
    xi = lax.rem(chip, 4)
    yi = lax.div(chip, 4)
    here = core * 8 + z

    def plane(o):
        dy, dx = o
        return (z, (lax.rem(yi + dy, 4) * 4 + lax.rem(xi + dx, 4)) * 2 + core)

    def column(o):
        dz, dc = o
        return (lax.rem(z + dz, 8), chip * 2 + lax.rem(core + dc, 2))

    def source_row(k):
        dy, dx = lax.div(k, 4), lax.rem(k, 4)
        return lax.rem(yi + 4 - dy, 4) * 4 + lax.rem(xi + 4 - dx, 4)

    def target_slot(r, dc):
        return (r // 4) * 8 + dc * 4 + r % 4

    def target_row(t):
        r = lax.div(t, 8) * 4 + lax.rem(t, 4)
        dc = lax.rem(lax.div(t, 4), 2)
        odd = lax.rem(r, 2)
        dz = odd * lax.div(r + 1, 2) + (1 - odd) * (8 - lax.div(r, 2))
        return lax.rem(core + dc, 2) * 8 + lax.rem(z + 16 - dz, 8)

    sibling = column((0, 1))

    def send(src, dst, ssem, rsem, dev):
        copy = pltpu.make_async_remote_copy(
            src_ref=src, dst_ref=dst, send_sem=ssem, recv_sem=rsem, device_id=dev, device_id_type=MESH
        )
        copy.start()

    def wait(ref, sem):
        pltpu.make_async_copy(ref, ref, sem).wait()

    barrier = pltpu.get_barrier_semaphore()
    for o in PLANE:
        pl.semaphore_signal(barrier, inc=1, device_id=plane(o), device_id_type=MESH)
    for o in COLUMN:
        pl.semaphore_signal(barrier, inc=1, device_id=column(o), device_id_type=MESH)
    loads = [
        pltpu.make_async_copy(src, dst, in_sem.at[k])
        for k, (src, dst) in enumerate([(x_ref, xs.at[0]), (y_ref, ys.at[0]), (b_ref, bown), (a_ref, av)])
    ]
    for load in loads:
        load.start()
    ones = (lax.broadcasted_iota(jnp.int32, (D, B), 0) < 3).astype(BF16)
    left = lax.broadcasted_iota(jnp.int32, (B, B), 1) < D
    for load in loads:
        load.wait()
    pl.semaphore_wait(barrier, len(PLANE) + len(COLUMN))

    def send_points(e, rings, slots):
        for r in rings:
            send(ys.at[0], ys.at[target_slot(r, 0)], y_send.at[e], y_recv.at[r], column((RING[r - 1], 0)))
        for k in slots:
            send(xs.at[0], xs.at[k], x_send.at[e], x_recv.at[k], plane((k // 4, k % 4)))

    send_points(0, (1, 2, 3), range(1, 8))
    send(ys.at[0], ys.at[target_slot(0, 1)], p_send, p_recv.at[0], sibling)
    send(bown, bsib, b_sem.at[0], b_sem.at[1], sibling)
    wait(ys.at[pl.ds(0, 3)], y_send.at[0])
    wait(xs.at[pl.ds(0, 7)], x_send.at[0])
    send_points(1, (4, 5, 6, 7), range(8, 16))

    def forward(r):
        slot = target_slot(r, 0)
        wait(ys.at[slot], y_recv.at[r])
        send(ys.at[slot], ys.at[target_slot(r, 1)], p_send, p_recv.at[r], sibling)

    def build_source(k):
        x = xs[k]
        xn[pl.ds(source_row(k), 1), :] = jnp.sum(x * x, axis=0, keepdims=True)
        scaled = x * (2.0 * SCORE)
        hi = scaled.astype(BF16)
        lo = (scaled - hi.astype(F32)).astype(BF16)
        at = slice(k * B, k * B + B)
        X[0:64, at] = hi
        X[64:128, at] = ones
        X[128:192, at] = hi
        X[192:256, at] = lo

    def build_target(t):
        y = ys[t]
        row = target_row(t)
        norm = jnp.sum(y * y, axis=0, keepdims=True)
        yn[pl.ds(row, 1), :] = norm
        mass = (bsib if t % 8 >= 4 else bown)[pl.ds(lax.rem(row, 8), 1), :] * LOG2E
        ba[pl.ds(row, 1), :] = mass
        bias = mass - norm * SCORE
        gb[pl.ds(row, 1), :] = bias
        hi = bias.astype(BF16).astype(F32)
        mid = (bias - hi).astype(BF16).astype(F32)
        lo = bias - hi - mid
        at8 = lax.broadcasted_iota(jnp.int32, (D, B), 0)
        tail = jnp.where(at8 == 0, hi, jnp.where(at8 == 1, mid, jnp.where(at8 == 2, lo, 0.0)))
        both = jnp.concatenate([y, tail], axis=0).T
        top = both.astype(BF16).astype(F32)
        rest = jnp.where(left, both - top, pltpu.roll(top, D, 1))
        at = slice(t * B, t * B + B)
        Y[at, 0:128] = top.astype(BF16)
        Y[at, 128:256] = rest.astype(BF16)

    def scores(r0, rn, c0, cn, fresh):
        step = 256

        def chunk(n, _):
            at = pl.ds(pl.multiple_of(c0 + n * 2 * step, 2 * step), 2 * step)
            Tb = T.at[r0 : r0 + rn, at]
            Mb, Sb = MS.at[0, :, at], MS.at[1, :, at]
            Xb = X.at[:, at]
            for h in range(2):
                half = slice(h * step, h * step + step)
                Tb[:, half] = jnp.dot(Y[r0 : r0 + rn, :], Xb[:, half], preferred_element_type=F32)
            for u in range(2 * step // B):
                lane = slice(u * B, u * B + B)
                m = s = None
                if not fresh:
                    m, s = Mb[:, lane], Sb[:, lane]
                for q in range(rn // B):
                    rows = [Tb[q * B + r * 8 : q * B + r * 8 + 8, lane] for r in range(16)]
                    new = tree(jnp.maximum, rows)
                    if m is not None:
                        new = jnp.maximum(m, new)
                    total = tree(jnp.add, [jnp.exp2(r - new) for r in rows])
                    s = total if m is None else total + s * jnp.exp2(m - new)
                    m = new
                Mb[:, lane] = m
                Sb[:, lane] = s
            return 0

        lax.fori_loop(0, cn // (2 * step), chunk, 0)

    H = N // 2
    Q = N // 4
    for r in (1, 2, 3):
        forward(r)
    for k in range(1, 8):
        wait(xs.at[k], x_recv.at[k])
    wait(bsib, b_sem.at[1])
    for k in range(8):
        build_source(k)
    for t in range(4):
        build_target(t)
    scores(0, Q, 0, H, True)
    for r in range(4):
        wait(ys.at[0], p_recv.at[r])
    for t in range(4, 8):
        build_target(t)
    scores(Q, Q, 0, H, False)
    for r in (4, 5, 6, 7):
        forward(r)
    for k in range(8, 16):
        wait(xs.at[k], x_recv.at[k])
    for k in range(8, 16):
        build_source(k)
    scores(0, H, H, H, True)
    for t in range(8, 12):
        build_target(t)
    scores(H, Q, 0, N, False)
    for r in range(4, 8):
        wait(ys.at[0], p_recv.at[r])
    for t in range(12, 16):
        build_target(t)
    scores(H + Q, Q, 0, N, False)
    for k in range(NB):
        lane = slice(k * B, k * B + B)
        m, s = MS[0, :, lane], MS[1, :, lane]
        top = jnp.max(m, axis=0, keepdims=True)
        total = jnp.sum(s * jnp.exp2(m - top), axis=0, keepdims=True)
        ex1[chip, pl.ds(source_row(k), 1), :] = top + jnp.log(total) * LOG2E

    def exchange(ex, mine, targets, e):
        for o in targets:
            send(ex.at[mine], ex.at[mine], e_send.at[e], e_recv.at[e], o)
        wait(ex.at[pl.ds(0, 15)], e_recv.at[e])

    planes = [plane(o) for o in FAR]
    columns = [column(o) for o in reversed(COLUMN)]

    exchange(ex1, chip, planes, 0)
    a2 = av[pl.ds(core, NB, stride=2), :] * LOG2E
    first = a2 - lse_rows(ex1[...])
    fa[...] = first
    for n in range(NB):
        fb8[:, n * B : (n + 1) * B] = jnp.broadcast_to(fa[pl.ds(source_row(n), 1), :], (8, B))

    def half2(t, _):
        block = pl.ds(pl.multiple_of(t * B, B), B)
        Tb, mb, sb = T.at[block], mbuf.at[block], sbuf.at[block]
        for q in range(NB):
            at = slice(q * 8, q * 8 + 8)
            parts = []
            for n in range(NB):
                lane = slice(n * B, (n + 1) * B)
                value = Tb[at, lane] + fb8[:, lane]
                Tb[at, lane] = value
                parts.append(value)
            top = tree(jnp.maximum, parts)
            mb[at, :] = top
            sb[at, :] = tree(jnp.add, [jnp.exp2(p - top) for p in parts])
        return 0

    lax.fori_loop(0, NB, half2, 0)

    for t in range(NB):
        at = slice(t * B, t * B + B)
        m = mbuf[at, :].T
        s = sbuf[at, :].T
        top = jnp.max(m, axis=0, keepdims=True)
        total = jnp.sum(s * jnp.exp2(m - top), axis=0, keepdims=True)
        ex2[here, pl.ds(target_row(t), 1), :] = top + jnp.log(total) * LOG2E

    exchange(ex2, here, columns, 1)
    b2 = ba[...]
    total2 = lse_rows(ex2[...])
    gb[...] = gb[...] - total2 + b2
    fa[...] = b2 - total2

    R8[...] = jnp.zeros((8, N), F32)

    for t in range(NB):
        mbuf[t * B : t * B + B, :] = jnp.broadcast_to(fa[pl.ds(target_row(t), 1), :], (B, B)).T

    def half3(t, _):
        block = pl.ds(pl.multiple_of(t * B, B), B)
        Tb, mb = T.at[block], mbuf.at[block]
        for h in range(2):
            ats = [slice((h * 8 + q) * 8, (h * 8 + q) * 8 + 8) for q in range(8)]
            shifts = [mb[at, :] for at in ats]
            for n in range(NB):
                lane = slice(n * B, (n + 1) * B)
                values = []
                for at, shift in zip(ats, shifts):
                    value = jnp.exp2(Tb[at, lane] + shift)
                    Tb[at, lane] = value
                    values.append(value)
                R8[:, lane] = R8[:, lane] + tree(jnp.add, values)
        return 0

    lax.fori_loop(0, NB, half3, 0)
    for n in range(NB):
        ex3[chip, pl.ds(source_row(n), 1), :] = jnp.sum(R8[:, n * B : (n + 1) * B], axis=0, keepdims=True)
    exchange(ex3, chip, planes, 2)
    total3 = jnp.sum(ex3[...], axis=0)
    second = first - jnp.log(total3) * LOG2E
    fsib[0] = xn[...] + second * UNIT
    send(fsib.at[0], fsib.at[1], f_sem.at[0], f_sem.at[1], sibling)
    fa[...] = jnp.exp2(a2) / total3
    for n in range(NB):
        v8[:, n * B : (n + 1) * B] = jnp.broadcast_to(fa[pl.ds(source_row(n), 1), :], (8, B))

    def half4(t, _):
        block = pl.ds(pl.multiple_of(t * B, B), B)
        Tb, sb = T.at[block], sbuf.at[block]
        for h in range(2):
            ats = [slice((h * 8 + q) * 8, (h * 8 + q) * 8 + 8) for q in range(8)]
            sums = [None] * 8
            for n in range(NB):
                lane = slice(n * B, (n + 1) * B)
                weight = v8[:, lane]
                for q, at in enumerate(ats):
                    value = Tb[at, lane] * weight
                    sums[q] = value if n == 0 else sums[q] + value
            for q, at in enumerate(ats):
                sb[at, :] = sums[q]
        return 0

    lax.fori_loop(0, NB, half4, 0)

    for t in range(NB):
        total = jnp.sum(sbuf[t * B : t * B + B, :].T, axis=0, keepdims=True)
        ex4[here, pl.ds(target_row(t), 1), :] = total

    exchange(ex4, here, columns, 3)
    total4 = jnp.sum(ex4[...], axis=0)
    fa[...] = yn[...] + (gb[...] - jnp.log(total4) * LOG2E) * UNIT
    g_ref[...] = fa[pl.ds(pl.multiple_of(core * 8, 8), 8), :]
    wait(fsib.at[1], f_sem.at[1])
    f_ref[pl.ds(core, NB, stride=2), :] = fsib[0]
    f_ref[pl.ds(1 - core, NB, stride=2), :] = fsib[1]

    wait(xs.at[pl.ds(0, 8)], x_send.at[1])
    wait(ys.at[pl.ds(0, 4)], y_send.at[1])
    wait(ys.at[pl.ds(0, 8)], p_send)
    wait(bown, b_sem.at[0])
    wait(fsib.at[0], f_sem.at[0])
    for e, ex in enumerate((ex1, ex2, ex3, ex4)):
        wait(ex.at[pl.ds(0, 15)], e_send.at[e])


def on_device(src_points, tgt_points, src_logmass, tgt_logmass):
    vmem = pl.BlockSpec(memory_space=pltpu.VMEM)
    dma = pltpu.SemaphoreType.DMA
    exchange = pltpu.VMEM((NB, NB, B), F32)
    f, g = pl.pallas_call(
        kernel,
        out_shape=(jax.ShapeDtypeStruct((32, B), F32), jax.ShapeDtypeStruct((8, B), F32)),
        in_specs=[pl.BlockSpec(memory_space=pl.ANY)] * 4,
        out_specs=(vmem, vmem),
        scratch_shapes=[
            pltpu.VMEM((NB, D, B), F32),
            pltpu.VMEM((NB, D, B), F32),
            pltpu.VMEM((32, B), F32),
            pltpu.VMEM((8, B), F32),
            pltpu.VMEM((8, B), F32),
            pltpu.VMEM((256, N), BF16),
            pltpu.VMEM((N, 256), BF16),
            pltpu.VMEM((N, N), F32),
            pltpu.VMEM((2, 8, N), F32),
            pltpu.VMEM((NB, B), F32),
            pltpu.VMEM((NB, B), F32),
            pltpu.VMEM((NB, B), F32),
            pltpu.VMEM((NB, B), F32),
            pltpu.VMEM((NB, B), F32),
            pltpu.VMEM((8, N), F32),
            pltpu.VMEM((N, B), F32),
            pltpu.VMEM((N, B), F32),
            pltpu.VMEM((8, N), F32),
            pltpu.VMEM((8, N), F32),
            exchange, exchange, exchange, exchange,
            pltpu.VMEM((2, NB, B), F32),
            dma((4,)), dma((2,)), dma((16,)), dma((2,)), dma((8,)), dma, dma((8,)), dma((2,)), dma((4,)), dma((4,)), dma((2,)),
        ],
        compiler_params=pltpu.CompilerParams(
            collective_id=0, has_side_effects=True, vmem_limit_bytes=56 << 20
        ),
    )(src_points, tgt_points, src_logmass.reshape(32, B), tgt_logmass.reshape(8, B))
    return f.reshape(-1), g.reshape(-1)


def solution(mesh):
    return jax.shard_map(
        on_device,
        mesh=mesh,
        in_specs=(P(None, ("row", "col")), P(None, ("col", "row")), P("row"), P("col")),
        out_specs=(P("row"), P("col")),
        check_vma=False,
    )
```

```python
import functools
import math

import jax
import jax.numpy as jnp
from jax import lax
from jax.experimental import pallas as pl
from jax.experimental.pallas import tpu as pltpu
from jax.sharding import PartitionSpec as P

MESH = pl.DeviceIdType.MESH
EPSILON = 0.05
LOG2E = math.log2(math.e)
SCORE = LOG2E / EPSILON
UNIT = EPSILON / LOG2E
D = 64
B = 128
NB = 16
N = NB * B
F32 = jnp.float32
BF16 = jnp.bfloat16

PLANE = [(dy, dx) for dy in range(4) for dx in range(4) if (dy, dx) != (0, 0)]
RING = [1, 7, 2, 6, 3, 5, 4]
COLUMN = sorted(
    [(dz, dc) for dz in range(8) for dc in range(2) if (dz, dc) != (0, 0)],
    key=lambda o: min(o[0], 8 - o[0]),
)
FAR = sorted(PLANE, key=lambda o: -min(o[0], 4 - o[0]) - min(o[1], 4 - o[1]))


def lse_rows(values):
    top = jnp.max(values, axis=0)
    return top + jnp.log(jnp.sum(jnp.exp2(values - top[None]), axis=0)) * LOG2E


def tree(op, parts):
    while len(parts) > 1:
        parts = [op(p, q) for p, q in zip(parts[::2], parts[1::2])]
    return parts[0]


def kernel(
    x_ref, y_ref, a_ref, b_ref, f_ref, g_ref,
    xs, ys, av, bown, bsib, X, Y, T, MS, xn, yn, gb, ba, fa, fb8, mbuf, sbuf, R8, v8,
    ex1, ex2, ex3, ex4, fsib,
    in_sem, x_send, x_recv, y_send, y_recv, p_send, p_recv, b_sem, e_send, e_recv, f_sem,
):
    z = lax.axis_index("row")
    c = lax.axis_index("col")
    core = lax.rem(c, 2)
    chip = lax.div(c, 2)
    xi = lax.rem(chip, 4)
    yi = lax.div(chip, 4)
    here = core * 8 + z

    def plane(o):
        dy, dx = o
        return (z, (lax.rem(yi + dy, 4) * 4 + lax.rem(xi + dx, 4)) * 2 + core)

    def column(o):
        dz, dc = o
        return (lax.rem(z + dz, 8), chip * 2 + lax.rem(core + dc, 2))

    def source_row(k):
        dy, dx = lax.div(k, 4), lax.rem(k, 4)
        return lax.rem(yi + 4 - dy, 4) * 4 + lax.rem(xi + 4 - dx, 4)

    def target_slot(r, dc):
        return (r // 4) * 8 + dc * 4 + r % 4

    def target_row(t):
        r = lax.div(t, 8) * 4 + lax.rem(t, 4)
        dc = lax.rem(lax.div(t, 4), 2)
        odd = lax.rem(r, 2)
        dz = odd * lax.div(r + 1, 2) + (1 - odd) * (8 - lax.div(r, 2))
        return lax.rem(core + dc, 2) * 8 + lax.rem(z + 16 - dz, 8)

    sibling = column((0, 1))

    def send(src, dst, ssem, rsem, dev):
        copy = pltpu.make_async_remote_copy(
            src_ref=src, dst_ref=dst, send_sem=ssem, recv_sem=rsem, device_id=dev, device_id_type=MESH
        )
        copy.start()

    def wait(ref, sem):
        pltpu.make_async_copy(ref, ref, sem).wait()

    barrier = pltpu.get_barrier_semaphore()
    for o in PLANE:
        pl.semaphore_signal(barrier, inc=1, device_id=plane(o), device_id_type=MESH)
    for o in COLUMN:
        pl.semaphore_signal(barrier, inc=1, device_id=column(o), device_id_type=MESH)
    loads = [
        pltpu.make_async_copy(src, dst, in_sem.at[k])
        for k, (src, dst) in enumerate([(x_ref, xs.at[0]), (y_ref, ys.at[0]), (b_ref, bown), (a_ref, av)])
    ]
    for load in loads:
        load.start()
    ones = (lax.broadcasted_iota(jnp.int32, (D, B), 0) < 3).astype(BF16)
    left = lax.broadcasted_iota(jnp.int32, (B, B), 1) < D
    for load in loads:
        load.wait()
    pl.semaphore_wait(barrier, len(PLANE) + len(COLUMN))

    def send_points(e, rings, slots):
        for r in rings:
            send(ys.at[0], ys.at[target_slot(r, 0)], y_send.at[e], y_recv.at[r], column((RING[r - 1], 0)))
        for k in slots:
            send(xs.at[0], xs.at[k], x_send.at[e], x_recv.at[k], plane((k // 4, k % 4)))

    send_points(0, (1, 2, 3), range(1, 8))
    send(ys.at[0], ys.at[target_slot(0, 1)], p_send, p_recv.at[0], sibling)
    send(bown, bsib, b_sem.at[0], b_sem.at[1], sibling)
    wait(ys.at[pl.ds(0, 3)], y_send.at[0])
    wait(xs.at[pl.ds(0, 7)], x_send.at[0])
    send_points(1, (4, 5, 6, 7), range(8, 16))

    def forward(r):
        slot = target_slot(r, 0)
        wait(ys.at[slot], y_recv.at[r])
        send(ys.at[slot], ys.at[target_slot(r, 1)], p_send, p_recv.at[r], sibling)

    def build_source(k):
        x = xs[k]
        xn[pl.ds(source_row(k), 1), :] = jnp.sum(x * x, axis=0, keepdims=True)
        scaled = x * (2.0 * SCORE)
        hi = scaled.astype(BF16)
        lo = (scaled - hi.astype(F32)).astype(BF16)
        at = slice(k * B, k * B + B)
        X[0:64, at] = hi
        X[64:128, at] = ones
        X[128:192, at] = hi
        X[192:256, at] = lo

    def build_target(t):
        y = ys[t]
        row = target_row(t)
        norm = jnp.sum(y * y, axis=0, keepdims=True)
        yn[pl.ds(row, 1), :] = norm
        mass = (bsib if t % 8 >= 4 else bown)[pl.ds(lax.rem(row, 8), 1), :] * LOG2E
        ba[pl.ds(row, 1), :] = mass
        bias = mass - norm * SCORE
        gb[pl.ds(row, 1), :] = bias
        hi = bias.astype(BF16).astype(F32)
        mid = (bias - hi).astype(BF16).astype(F32)
        lo = bias - hi - mid
        at8 = lax.broadcasted_iota(jnp.int32, (D, B), 0)
        tail = jnp.where(at8 == 0, hi, jnp.where(at8 == 1, mid, jnp.where(at8 == 2, lo, 0.0)))
        both = jnp.concatenate([y, tail], axis=0).T
        top = both.astype(BF16).astype(F32)
        rest = jnp.where(left, both - top, pltpu.roll(top, D, 1))
        at = slice(t * B, t * B + B)
        Y[at, 0:128] = top.astype(BF16)
        Y[at, 128:256] = rest.astype(BF16)

    def scores(r0, rn, c0, cn, fresh):
        step = 256
        width = cn // 2

        def chunk(n, _):
            at = pl.ds(pl.multiple_of(c0 + n * width, width), width)
            Tb = T.at[r0 : r0 + rn, at]
            Mb, Sb = MS.at[0, :, at], MS.at[1, :, at]
            Xb = X.at[:, at]
            for h in range(width // step):
                half = slice(h * step, h * step + step)
                Tb[:, half] = jnp.dot(Y[r0 : r0 + rn, :], Xb[:, half], preferred_element_type=F32)
            for u in range(width // B):
                lane = slice(u * B, u * B + B)
                m = s = None
                if not fresh:
                    m, s = Mb[:, lane], Sb[:, lane]
                for q in range(rn // B):
                    rows = [Tb[q * B + r * 8 : q * B + r * 8 + 8, lane] for r in range(16)]
                    new = tree(jnp.maximum, rows)
                    if m is not None:
                        new = jnp.maximum(m, new)
                    total = tree(jnp.add, [jnp.exp2(r - new) for r in rows])
                    s = total if m is None else total + s * jnp.exp2(m - new)
                    m = new
                Mb[:, lane] = m
                Sb[:, lane] = s
            return 0

        lax.fori_loop(0, 2, chunk, 0)

    H = N // 2
    Q = N // 4
    for r in (1, 2, 3):
        forward(r)
    for k in range(1, 8):
        wait(xs.at[k], x_recv.at[k])
    wait(bsib, b_sem.at[1])
    for k in range(8):
        build_source(k)
    for t in range(4):
        build_target(t)
    scores(0, Q, 0, H, True)
    for r in range(4):
        wait(ys.at[0], p_recv.at[r])
    for t in range(4, 8):
        build_target(t)
    scores(Q, Q, 0, H, False)
    for r in (4, 5, 6, 7):
        forward(r)
    for k in range(8, 16):
        wait(xs.at[k], x_recv.at[k])
    for k in range(8, 16):
        build_source(k)
    scores(0, H, H, H, True)
    for t in range(8, 12):
        build_target(t)
    scores(H, Q, 0, N, False)
    for r in range(4, 8):
        wait(ys.at[0], p_recv.at[r])
    for t in range(12, 16):
        build_target(t)
    scores(H + Q, Q, 0, N, False)
    for k in range(NB):
        lane = slice(k * B, k * B + B)
        m, s = MS[0, :, lane], MS[1, :, lane]
        top = jnp.max(m, axis=0, keepdims=True)
        total = jnp.sum(s * jnp.exp2(m - top), axis=0, keepdims=True)
        ex1[chip, pl.ds(source_row(k), 1), :] = top + jnp.log(total) * LOG2E

    def exchange(ex, mine, targets, e):
        for o in targets:
            send(ex.at[mine], ex.at[mine], e_send.at[e], e_recv.at[e], o)
        wait(ex.at[pl.ds(0, 15)], e_recv.at[e])

    planes = [plane(o) for o in FAR]
    columns = [column(o) for o in reversed(COLUMN)]

    exchange(ex1, chip, planes, 0)
    a2 = av[pl.ds(core, NB, stride=2), :] * LOG2E
    first = a2 - lse_rows(ex1[...])
    fa[...] = first
    for n in range(NB):
        fb8[:, n * B : (n + 1) * B] = jnp.broadcast_to(fa[pl.ds(source_row(n), 1), :], (8, B))

    def half2(t, _):
        block = pl.ds(pl.multiple_of(t * B, B), B)
        Tb, mb, sb = T.at[block], mbuf.at[block], sbuf.at[block]
        for q in range(NB):
            at = slice(q * 8, q * 8 + 8)
            parts = []
            for n in range(NB):
                lane = slice(n * B, (n + 1) * B)
                value = Tb[at, lane] + fb8[:, lane]
                Tb[at, lane] = value
                parts.append(value)
            top = tree(jnp.maximum, parts)
            mb[at, :] = top
            sb[at, :] = tree(jnp.add, [jnp.exp2(p - top) for p in parts])
        return 0

    lax.fori_loop(0, NB, half2, 0)

    for t in range(NB):
        at = slice(t * B, t * B + B)
        m = mbuf[at, :].T
        s = sbuf[at, :].T
        top = jnp.max(m, axis=0, keepdims=True)
        total = jnp.sum(s * jnp.exp2(m - top), axis=0, keepdims=True)
        ex2[here, pl.ds(target_row(t), 1), :] = top + jnp.log(total) * LOG2E

    exchange(ex2, here, columns, 1)
    b2 = ba[...]
    total2 = lse_rows(ex2[...])
    gb[...] = gb[...] - total2 + b2
    fa[...] = b2 - total2

    R8[...] = jnp.zeros((8, N), F32)

    for t in range(NB):
        mbuf[t * B : t * B + B, :] = jnp.broadcast_to(fa[pl.ds(target_row(t), 1), :], (B, B)).T

    def half3(t, _):
        block = pl.ds(pl.multiple_of(t * B, B), B)
        Tb, mb = T.at[block], mbuf.at[block]
        for h in range(2):
            ats = [slice((h * 8 + q) * 8, (h * 8 + q) * 8 + 8) for q in range(8)]
            shifts = [mb[at, :] for at in ats]
            for n in range(NB):
                lane = slice(n * B, (n + 1) * B)
                values = []
                for at, shift in zip(ats, shifts):
                    value = jnp.exp2(Tb[at, lane] + shift)
                    Tb[at, lane] = value
                    values.append(value)
                R8[:, lane] = R8[:, lane] + tree(jnp.add, values)
        return 0

    lax.fori_loop(0, NB, half3, 0)
    for n in range(NB):
        ex3[chip, pl.ds(source_row(n), 1), :] = jnp.sum(R8[:, n * B : (n + 1) * B], axis=0, keepdims=True)
    exchange(ex3, chip, planes, 2)
    total3 = jnp.sum(ex3[...], axis=0)
    second = first - jnp.log(total3) * LOG2E
    fsib[0] = xn[...] + second * UNIT
    send(fsib.at[0], fsib.at[1], f_sem.at[0], f_sem.at[1], sibling)
    fa[...] = jnp.exp2(a2) / total3
    for n in range(NB):
        v8[:, n * B : (n + 1) * B] = jnp.broadcast_to(fa[pl.ds(source_row(n), 1), :], (8, B))

    def half4(t, _):
        block = pl.ds(pl.multiple_of(t * B, B), B)
        Tb, sb = T.at[block], sbuf.at[block]
        for h in range(2):
            ats = [slice((h * 8 + q) * 8, (h * 8 + q) * 8 + 8) for q in range(8)]
            sums = [None] * 8
            for n in range(NB):
                lane = slice(n * B, (n + 1) * B)
                weight = v8[:, lane]
                for q, at in enumerate(ats):
                    value = Tb[at, lane] * weight
                    sums[q] = value if n == 0 else sums[q] + value
            for q, at in enumerate(ats):
                sb[at, :] = sums[q]
        return 0

    lax.fori_loop(0, NB, half4, 0)

    for t in range(NB):
        total = jnp.sum(sbuf[t * B : t * B + B, :].T, axis=0, keepdims=True)
        ex4[here, pl.ds(target_row(t), 1), :] = total

    exchange(ex4, here, columns, 3)
    total4 = jnp.sum(ex4[...], axis=0)
    fa[...] = yn[...] + (gb[...] - jnp.log(total4) * LOG2E) * UNIT
    g_ref[...] = fa[pl.ds(pl.multiple_of(core * 8, 8), 8), :]
    wait(fsib.at[1], f_sem.at[1])
    f_ref[pl.ds(core, NB, stride=2), :] = fsib[0]
    f_ref[pl.ds(1 - core, NB, stride=2), :] = fsib[1]

    wait(xs.at[pl.ds(0, 8)], x_send.at[1])
    wait(ys.at[pl.ds(0, 4)], y_send.at[1])
    wait(ys.at[pl.ds(0, 8)], p_send)
    wait(bown, b_sem.at[0])
    wait(fsib.at[0], f_sem.at[0])
    for e, ex in enumerate((ex1, ex2, ex3, ex4)):
        wait(ex.at[pl.ds(0, 15)], e_send.at[e])


def on_device(src_points, tgt_points, src_logmass, tgt_logmass):
    vmem = pl.BlockSpec(memory_space=pltpu.VMEM)
    dma = pltpu.SemaphoreType.DMA
    exchange = pltpu.VMEM((NB, NB, B), F32)
    f, g = pl.pallas_call(
        kernel,
        out_shape=(jax.ShapeDtypeStruct((32, B), F32), jax.ShapeDtypeStruct((8, B), F32)),
        in_specs=[pl.BlockSpec(memory_space=pl.ANY)] * 4,
        out_specs=(vmem, vmem),
        scratch_shapes=[
            pltpu.VMEM((NB, D, B), F32),
            pltpu.VMEM((NB, D, B), F32),
            pltpu.VMEM((32, B), F32),
            pltpu.VMEM((8, B), F32),
            pltpu.VMEM((8, B), F32),
            pltpu.VMEM((256, N), BF16),
            pltpu.VMEM((N, 256), BF16),
            pltpu.VMEM((N, N), F32),
            pltpu.VMEM((2, 8, N), F32),
            pltpu.VMEM((NB, B), F32),
            pltpu.VMEM((NB, B), F32),
            pltpu.VMEM((NB, B), F32),
            pltpu.VMEM((NB, B), F32),
            pltpu.VMEM((NB, B), F32),
            pltpu.VMEM((8, N), F32),
            pltpu.VMEM((N, B), F32),
            pltpu.VMEM((N, B), F32),
            pltpu.VMEM((8, N), F32),
            pltpu.VMEM((8, N), F32),
            exchange, exchange, exchange, exchange,
            pltpu.VMEM((2, NB, B), F32),
            dma((4,)), dma((2,)), dma((16,)), dma((2,)), dma((8,)), dma, dma((8,)), dma((2,)), dma((4,)), dma((4,)), dma((2,)),
        ],
        compiler_params=pltpu.CompilerParams(
            collective_id=0, has_side_effects=True, vmem_limit_bytes=56 << 20
        ),
    )(src_points, tgt_points, src_logmass.reshape(32, B), tgt_logmass.reshape(8, B))
    return f.reshape(-1), g.reshape(-1)


def solution(mesh):
    return jax.shard_map(
        on_device,
        mesh=mesh,
        in_specs=(P(None, ("row", "col")), P(None, ("col", "row")), P("row"), P("col")),
        out_specs=(P("row"), P("col")),
        check_vma=False,
    )
```

```python
import functools
import math

import jax
import jax.numpy as jnp
from jax import lax
from jax.experimental import pallas as pl
from jax.experimental.pallas import tpu as pltpu
from jax.sharding import PartitionSpec as P

MESH = pl.DeviceIdType.MESH
EPSILON = 0.05
LOG2E = math.log2(math.e)
SCORE = LOG2E / EPSILON
UNIT = EPSILON / LOG2E
D = 64
B = 128
NB = 16
N = NB * B
F32 = jnp.float32
BF16 = jnp.bfloat16

PLANE = [(dy, dx) for dy in range(4) for dx in range(4) if (dy, dx) != (0, 0)]
RING = [1, 7, 2, 6, 3, 5, 4]
COLUMN = sorted(
    [(dz, dc) for dz in range(8) for dc in range(2) if (dz, dc) != (0, 0)],
    key=lambda o: min(o[0], 8 - o[0]),
)
FAR = sorted(PLANE, key=lambda o: -min(o[0], 4 - o[0]) - min(o[1], 4 - o[1]))


def lse_rows(values):
    top = jnp.max(values, axis=0)
    return top + jnp.log(jnp.sum(jnp.exp2(values - top[None]), axis=0)) * LOG2E


def tree(op, parts):
    while len(parts) > 1:
        parts = [op(p, q) for p, q in zip(parts[::2], parts[1::2])]
    return parts[0]


def kernel(
    x_ref, y_ref, a_ref, b_ref, f_ref, g_ref,
    xs, ys, av, bown, bsib, X, Y, T, MS, xn, yn, gb, ba, fa, fb8, mbuf, sbuf, R8, v8,
    ex1, ex2, ex3, ex4, fsib,
    in_sem, x_send, x_recv, y_send, y_recv, p_send, p_recv, b_sem, e_send, e_recv, r_send, r_recv, f_sem,
):
    z = lax.axis_index("row")
    c = lax.axis_index("col")
    core = lax.rem(c, 2)
    chip = lax.div(c, 2)
    xi = lax.rem(chip, 4)
    yi = lax.div(chip, 4)
    here = core * 8 + z

    def plane(o):
        dy, dx = o
        return (z, (lax.rem(yi + dy, 4) * 4 + lax.rem(xi + dx, 4)) * 2 + core)

    def column(o):
        dz, dc = o
        return (lax.rem(z + dz, 8), chip * 2 + lax.rem(core + dc, 2))

    def source_row(k):
        dy, dx = lax.div(k, 4), lax.rem(k, 4)
        return lax.rem(yi + 4 - dy, 4) * 4 + lax.rem(xi + 4 - dx, 4)

    def target_slot(r, dc):
        return (r // 4) * 8 + dc * 4 + r % 4

    def target_row(t):
        r = lax.div(t, 8) * 4 + lax.rem(t, 4)
        dc = lax.rem(lax.div(t, 4), 2)
        odd = lax.rem(r, 2)
        dz = odd * lax.div(r + 1, 2) + (1 - odd) * (8 - lax.div(r, 2))
        return lax.rem(core + dc, 2) * 8 + lax.rem(z + 16 - dz, 8)

    sibling = column((0, 1))

    def send(src, dst, ssem, rsem, dev):
        copy = pltpu.make_async_remote_copy(
            src_ref=src, dst_ref=dst, send_sem=ssem, recv_sem=rsem, device_id=dev, device_id_type=MESH
        )
        copy.start()

    def wait(ref, sem):
        pltpu.make_async_copy(ref, ref, sem).wait()

    barrier = pltpu.get_barrier_semaphore()
    for o in PLANE:
        pl.semaphore_signal(barrier, inc=1, device_id=plane(o), device_id_type=MESH)
    for o in COLUMN:
        pl.semaphore_signal(barrier, inc=1, device_id=column(o), device_id_type=MESH)
    loads = [
        pltpu.make_async_copy(src, dst, in_sem.at[k])
        for k, (src, dst) in enumerate([(x_ref, xs.at[0]), (y_ref, ys.at[0]), (b_ref, bown), (a_ref, av)])
    ]
    for load in loads:
        load.start()
    ones = (lax.broadcasted_iota(jnp.int32, (D, B), 0) < 3).astype(BF16)
    left = lax.broadcasted_iota(jnp.int32, (B, B), 1) < D
    for load in loads:
        load.wait()
    pl.semaphore_wait(barrier, len(PLANE) + len(COLUMN))

    def send_points(e, rings, slots):
        for r in rings:
            send(ys.at[0], ys.at[target_slot(r, 0)], y_send.at[e], y_recv.at[r], column((RING[r - 1], 0)))
        for k in slots:
            send(xs.at[0], xs.at[k], x_send.at[e], x_recv.at[k], plane((k // 4, k % 4)))

    send_points(0, (1, 2, 3), range(1, 8))
    send(ys.at[0], ys.at[target_slot(0, 1)], p_send, p_recv.at[0], sibling)
    send(bown, bsib, b_sem.at[0], b_sem.at[1], sibling)
    wait(ys.at[pl.ds(0, 3)], y_send.at[0])
    wait(xs.at[pl.ds(0, 7)], x_send.at[0])
    send_points(1, (4, 5, 6, 7), range(8, 16))

    def forward(r):
        slot = target_slot(r, 0)
        wait(ys.at[slot], y_recv.at[r])
        send(ys.at[slot], ys.at[target_slot(r, 1)], p_send, p_recv.at[r], sibling)

    def build_source(k):
        x = xs[k]
        xn[pl.ds(source_row(k), 1), :] = jnp.sum(x * x, axis=0, keepdims=True)
        scaled = x * (2.0 * SCORE)
        hi = scaled.astype(BF16)
        lo = (scaled - hi.astype(F32)).astype(BF16)
        at = slice(k * B, k * B + B)
        X[0:64, at] = hi
        X[64:128, at] = ones
        X[128:192, at] = hi
        X[192:256, at] = lo

    def build_target(t):
        y = ys[t]
        row = target_row(t)
        norm = jnp.sum(y * y, axis=0, keepdims=True)
        yn[pl.ds(row, 1), :] = norm
        mass = (bsib if t % 8 >= 4 else bown)[pl.ds(lax.rem(row, 8), 1), :] * LOG2E
        ba[pl.ds(row, 1), :] = mass
        bias = mass - norm * SCORE
        gb[pl.ds(row, 1), :] = bias
        hi = bias.astype(BF16).astype(F32)
        mid = (bias - hi).astype(BF16).astype(F32)
        lo = bias - hi - mid
        at8 = lax.broadcasted_iota(jnp.int32, (D, B), 0)
        tail = jnp.where(at8 == 0, hi, jnp.where(at8 == 1, mid, jnp.where(at8 == 2, lo, 0.0)))
        both = jnp.concatenate([y, tail], axis=0).T
        top = both.astype(BF16).astype(F32)
        rest = jnp.where(left, both - top, pltpu.roll(top, D, 1))
        at = slice(t * B, t * B + B)
        Y[at, 0:128] = top.astype(BF16)
        Y[at, 128:256] = rest.astype(BF16)

    def scores(r0, rn, c0, cn, fresh):
        step = 256
        width = cn // 2

        def chunk(n, _):
            at = pl.ds(pl.multiple_of(c0 + n * width, width), width)
            Tb = T.at[r0 : r0 + rn, at]
            Mb, Sb = MS.at[0, :, at], MS.at[1, :, at]
            Xb = X.at[:, at]
            for h in range(width // step):
                half = slice(h * step, h * step + step)
                Tb[:, half] = jnp.dot(Y[r0 : r0 + rn, :], Xb[:, half], preferred_element_type=F32)
            for u in range(width // B):
                lane = slice(u * B, u * B + B)
                m = s = None
                if not fresh:
                    m, s = Mb[:, lane], Sb[:, lane]
                for q in range(rn // B):
                    rows = [Tb[q * B + r * 8 : q * B + r * 8 + 8, lane] for r in range(16)]
                    new = tree(jnp.maximum, rows)
                    if m is not None:
                        new = jnp.maximum(m, new)
                    total = tree(jnp.add, [jnp.exp2(r - new) for r in rows])
                    s = total if m is None else total + s * jnp.exp2(m - new)
                    m = new
                Mb[:, lane] = m
                Sb[:, lane] = s
            return 0

        lax.fori_loop(0, 2, chunk, 0)

    H = N // 2
    Q = N // 4
    for r in (1, 2, 3):
        forward(r)
    for k in range(1, 8):
        wait(xs.at[k], x_recv.at[k])
    wait(bsib, b_sem.at[1])
    for k in range(8):
        build_source(k)
    for t in range(4):
        build_target(t)
    scores(0, Q, 0, H, True)
    for r in range(4):
        wait(ys.at[0], p_recv.at[r])
    for t in range(4, 8):
        build_target(t)
    scores(Q, Q, 0, H, False)
    for r in (4, 5, 6, 7):
        forward(r)
    for k in range(8, 16):
        wait(xs.at[k], x_recv.at[k])
    for k in range(8, 16):
        build_source(k)
    scores(0, H, H, H, True)
    for t in range(8, 12):
        build_target(t)
    scores(H, Q, 0, N, False)
    for r in range(4, 8):
        wait(ys.at[0], p_recv.at[r])
    for t in range(12, 16):
        build_target(t)
    scores(H + Q, Q, 0, N, False)
    for k in range(NB):
        lane = slice(k * B, k * B + B)
        m, s = MS[0, :, lane], MS[1, :, lane]
        top = jnp.max(m, axis=0, keepdims=True)
        total = jnp.sum(s * jnp.exp2(m - top), axis=0, keepdims=True)
        ex1[chip, pl.ds(source_row(k), 1), :] = top + jnp.log(total) * LOG2E

    def exchange(ex, mine, targets, e):
        for o in targets:
            send(ex.at[mine], ex.at[mine], e_send.at[e], e_recv.at[e], o)
        wait(ex.at[pl.ds(0, 15)], e_recv.at[e])

    planes = [plane(o) for o in FAR]
    columns = [column(o) for o in reversed(COLUMN)]

    exchange(ex1, chip, planes, 0)
    a2 = av[pl.ds(core, NB, stride=2), :] * LOG2E
    first = a2 - lse_rows(ex1[...])
    fa[...] = first
    for n in range(NB):
        fb8[:, n * B : (n + 1) * B] = jnp.broadcast_to(fa[pl.ds(source_row(n), 1), :], (8, B))

    def half2(t, _):
        block = pl.ds(pl.multiple_of(t * B, B), B)
        Tb, mb, sb = T.at[block], mbuf.at[block], sbuf.at[block]
        for q in range(NB):
            at = slice(q * 8, q * 8 + 8)
            parts = []
            for n in range(NB):
                lane = slice(n * B, (n + 1) * B)
                value = Tb[at, lane] + fb8[:, lane]
                Tb[at, lane] = value
                parts.append(value)
            top = tree(jnp.maximum, parts)
            mb[at, :] = top
            sb[at, :] = tree(jnp.add, [jnp.exp2(p - top) for p in parts])
        return 0

    lax.fori_loop(0, NB, half2, 0)

    for t in range(NB):
        at = slice(t * B, t * B + B)
        m = mbuf[at, :].T
        s = sbuf[at, :].T
        top = jnp.max(m, axis=0, keepdims=True)
        total = jnp.sum(s * jnp.exp2(m - top), axis=0, keepdims=True)
        ex2[here, pl.ds(target_row(t), 1), :] = top + jnp.log(total) * LOG2E

    exchange(ex2, here, columns, 1)
    b2 = ba[...]
    total2 = lse_rows(ex2[...])
    gb[...] = gb[...] - total2 + b2
    fa[...] = b2 - total2

    R8[...] = jnp.zeros((8, N), F32)

    for t in range(NB):
        mbuf[t * B : t * B + B, :] = jnp.broadcast_to(fa[pl.ds(target_row(t), 1), :], (B, B)).T

    def lanes_of(my):
        return pl.ds(pl.multiple_of(lax.rem(yi + 4 - my, 4) * Q, Q), Q)

    for e in range(2):
        spans = [lanes_of(2 * e), lanes_of(2 * e + 1)]

        def half3(t, _):
            block = pl.ds(pl.multiple_of(t * B, B), B)
            mb = mbuf.at[block]
            for span in spans:
                Tb, Rb = T.at[block, span], R8.at[:, span]
                for h in range(2):
                    ats = [slice((h * 8 + q) * 8, (h * 8 + q) * 8 + 8) for q in range(8)]
                    shifts = [mb[at, :] for at in ats]
                    for n in range(4):
                        lane = slice(n * B, (n + 1) * B)
                        values = []
                        for at, shift in zip(ats, shifts):
                            value = jnp.exp2(Tb[at, lane] + shift)
                            Tb[at, lane] = value
                            values.append(value)
                        Rb[:, lane] = Rb[:, lane] + tree(jnp.add, values)
            return 0

        lax.fori_loop(0, NB, half3, 0)
        for g, span in enumerate(spans):
            Rb = R8.at[:, span]
            for n in range(4):
                row = (2 * e + g) * 4 + lax.rem(xi + 4 - n, 4)
                ex3[chip, pl.ds(row, 1), :] = jnp.sum(Rb[:, n * B : (n + 1) * B], axis=0, keepdims=True)
        part = ex3.at[chip, pl.ds(8 * e, 8)]
        for o in planes:
            send(part, part, r_send.at[e], r_recv.at[e], o)

    for e in range(2):
        wait(ex3.at[pl.ds(0, 15), pl.ds(0, 8)], r_recv.at[e])
        rows = slice(8 * e, 8 * e + 8)
        total3 = jnp.sum(ex3[:, rows, :], axis=0)
        fsib[0, rows, :] = xn[rows, :] + (first[rows] - jnp.log(total3) * LOG2E) * UNIT
        fa[rows, :] = jnp.exp2(a2[rows]) / total3
        spans = [lanes_of(2 * e), lanes_of(2 * e + 1)]
        for g, span in enumerate(spans):
            vb = v8.at[:, span]
            for n in range(4):
                row = (2 * e + g) * 4 + lax.rem(xi + 4 - n, 4)
                vb[:, n * B : (n + 1) * B] = jnp.broadcast_to(fa[pl.ds(row, 1), :], (8, B))
        if e == 1:
            send(fsib.at[0], fsib.at[1], f_sem.at[0], f_sem.at[1], sibling)

        def half4(t, _):
            block = pl.ds(pl.multiple_of(t * B, B), B)
            sb = sbuf.at[block]
            for h in range(2):
                ats = [slice((h * 8 + q) * 8, (h * 8 + q) * 8 + 8) for q in range(8)]
                sums = [sb[at, :] for at in ats] if e else [None] * 8
                for span in spans:
                    Tb, vb = T.at[block, span], v8.at[:, span]
                    for n in range(4):
                        lane = slice(n * B, (n + 1) * B)
                        weight = vb[:, lane]
                        for q, at in enumerate(ats):
                            value = Tb[at, lane] * weight
                            sums[q] = value if sums[q] is None else sums[q] + value
                for q, at in enumerate(ats):
                    sb[at, :] = sums[q]
            return 0

        lax.fori_loop(0, NB, half4, 0)

    for t in range(NB):
        total = jnp.sum(sbuf[t * B : t * B + B, :].T, axis=0, keepdims=True)
        ex4[here, pl.ds(target_row(t), 1), :] = total

    exchange(ex4, here, columns, 3)
    total4 = jnp.sum(ex4[...], axis=0)
    fa[...] = yn[...] + (gb[...] - jnp.log(total4) * LOG2E) * UNIT
    g_ref[...] = fa[pl.ds(pl.multiple_of(core * 8, 8), 8), :]
    wait(fsib.at[1], f_sem.at[1])
    f_ref[pl.ds(core, NB, stride=2), :] = fsib[0]
    f_ref[pl.ds(1 - core, NB, stride=2), :] = fsib[1]

    wait(xs.at[pl.ds(0, 8)], x_send.at[1])
    wait(ys.at[pl.ds(0, 4)], y_send.at[1])
    wait(ys.at[pl.ds(0, 8)], p_send)
    wait(bown, b_sem.at[0])
    wait(fsib.at[0], f_sem.at[0])
    for e in range(2):
        wait(ex3.at[pl.ds(0, 15), pl.ds(0, 8)], r_send.at[e])
    for e, ex in ((0, ex1), (1, ex2), (3, ex4)):
        wait(ex.at[pl.ds(0, 15)], e_send.at[e])


def on_device(src_points, tgt_points, src_logmass, tgt_logmass):
    vmem = pl.BlockSpec(memory_space=pltpu.VMEM)
    dma = pltpu.SemaphoreType.DMA
    exchange = pltpu.VMEM((NB, NB, B), F32)
    f, g = pl.pallas_call(
        kernel,
        out_shape=(jax.ShapeDtypeStruct((32, B), F32), jax.ShapeDtypeStruct((8, B), F32)),
        in_specs=[pl.BlockSpec(memory_space=pl.ANY)] * 4,
        out_specs=(vmem, vmem),
        scratch_shapes=[
            pltpu.VMEM((NB, D, B), F32),
            pltpu.VMEM((NB, D, B), F32),
            pltpu.VMEM((32, B), F32),
            pltpu.VMEM((8, B), F32),
            pltpu.VMEM((8, B), F32),
            pltpu.VMEM((256, N), BF16),
            pltpu.VMEM((N, 256), BF16),
            pltpu.VMEM((N, N), F32),
            pltpu.VMEM((2, 8, N), F32),
            pltpu.VMEM((NB, B), F32),
            pltpu.VMEM((NB, B), F32),
            pltpu.VMEM((NB, B), F32),
            pltpu.VMEM((NB, B), F32),
            pltpu.VMEM((NB, B), F32),
            pltpu.VMEM((8, N), F32),
            pltpu.VMEM((N, B), F32),
            pltpu.VMEM((N, B), F32),
            pltpu.VMEM((8, N), F32),
            pltpu.VMEM((8, N), F32),
            exchange, exchange, exchange, exchange,
            pltpu.VMEM((2, NB, B), F32),
            dma((4,)), dma((2,)), dma((16,)), dma((2,)), dma((8,)), dma, dma((8,)), dma((2,)), dma((4,)), dma((4,)), dma((2,)), dma((2,)), dma((2,)),
        ],
        compiler_params=pltpu.CompilerParams(
            collective_id=0, has_side_effects=True, vmem_limit_bytes=56 << 20
        ),
    )(src_points, tgt_points, src_logmass.reshape(32, B), tgt_logmass.reshape(8, B))
    return f.reshape(-1), g.reshape(-1)


def solution(mesh):
    return jax.shard_map(
        on_device,
        mesh=mesh,
        in_specs=(P(None, ("row", "col")), P(None, ("col", "row")), P("row"), P("col")),
        out_specs=(P("row"), P("col")),
        check_vma=False,
    )
```

```python
import functools
import math

import jax
import jax.numpy as jnp
from jax import lax
from jax.experimental import pallas as pl
from jax.experimental.pallas import tpu as pltpu
from jax.sharding import PartitionSpec as P

MESH = pl.DeviceIdType.MESH
EPSILON = 0.05
LOG2E = math.log2(math.e)
SCORE = LOG2E / EPSILON
UNIT = EPSILON / LOG2E
D = 64
B = 128
NB = 16
N = NB * B
F32 = jnp.float32
BF16 = jnp.bfloat16

PLANE = [(dy, dx) for dy in range(4) for dx in range(4) if (dy, dx) != (0, 0)]
RING = [1, 7, 2, 6, 3, 5, 4]
COLUMN = sorted(
    [(dz, dc) for dz in range(8) for dc in range(2) if (dz, dc) != (0, 0)],
    key=lambda o: min(o[0], 8 - o[0]),
)
FAR = sorted(PLANE, key=lambda o: -min(o[0], 4 - o[0]) - min(o[1], 4 - o[1]))


def lse_rows(values):
    top = jnp.max(values, axis=0)
    return top + jnp.log(jnp.sum(jnp.exp2(values - top[None]), axis=0)) * LOG2E


def tree(op, parts):
    while len(parts) > 1:
        parts = [op(p, q) for p, q in zip(parts[::2], parts[1::2])]
    return parts[0]


def kernel(
    x_ref, y_ref, a_ref, b_ref, f_ref, g_ref,
    xs, ys, av, bown, bsib, X, Y, T, MS, xn, yn, gb, ba, fa, fb8, mbuf, sbuf, R8, v8,
    ex1, ex2, ex3, ex4, fsib,
    in_sem, x_send, x_recv, y_send, y_recv, p_send, p_recv, b_sem, e_send, e_recv, r_send, r_recv, f_sem,
):
    z = lax.axis_index("row")
    c = lax.axis_index("col")
    core = lax.rem(c, 2)
    chip = lax.div(c, 2)
    xi = lax.rem(chip, 4)
    yi = lax.div(chip, 4)
    here = core * 8 + z

    def plane(o):
        dy, dx = o
        return (z, (lax.rem(yi + dy, 4) * 4 + lax.rem(xi + dx, 4)) * 2 + core)

    def column(o):
        dz, dc = o
        return (lax.rem(z + dz, 8), chip * 2 + lax.rem(core + dc, 2))

    def source_row(k):
        dy, dx = lax.div(k, 4), lax.rem(k, 4)
        return lax.rem(yi + 4 - dy, 4) * 4 + lax.rem(xi + 4 - dx, 4)

    def target_slot(r, dc):
        return (r // 4) * 8 + dc * 4 + r % 4

    def target_row(t):
        r = lax.div(t, 8) * 4 + lax.rem(t, 4)
        dc = lax.rem(lax.div(t, 4), 2)
        odd = lax.rem(r, 2)
        dz = odd * lax.div(r + 1, 2) + (1 - odd) * (8 - lax.div(r, 2))
        return lax.rem(core + dc, 2) * 8 + lax.rem(z + 16 - dz, 8)

    sibling = column((0, 1))

    def send(src, dst, ssem, rsem, dev):
        copy = pltpu.make_async_remote_copy(
            src_ref=src, dst_ref=dst, send_sem=ssem, recv_sem=rsem, device_id=dev, device_id_type=MESH
        )
        copy.start()

    def wait(ref, sem):
        pltpu.make_async_copy(ref, ref, sem).wait()

    barrier = pltpu.get_barrier_semaphore()
    for o in PLANE:
        pl.semaphore_signal(barrier, inc=1, device_id=plane(o), device_id_type=MESH)
    for o in COLUMN:
        pl.semaphore_signal(barrier, inc=1, device_id=column(o), device_id_type=MESH)
    loads = [
        pltpu.make_async_copy(src, dst, in_sem.at[k])
        for k, (src, dst) in enumerate([(x_ref, xs.at[0]), (y_ref, ys.at[0]), (b_ref, bown), (a_ref, av)])
    ]
    for load in loads:
        load.start()
    ones = (lax.broadcasted_iota(jnp.int32, (D, B), 0) < 3).astype(BF16)
    left = lax.broadcasted_iota(jnp.int32, (B, B), 1) < D
    for load in loads:
        load.wait()
    pl.semaphore_wait(barrier, len(PLANE) + len(COLUMN))

    def send_points(e, rings, slots):
        for r in rings:
            send(ys.at[0], ys.at[target_slot(r, 0)], y_send.at[e], y_recv.at[r], column((RING[r - 1], 0)))
        for k in slots:
            send(xs.at[0], xs.at[k], x_send.at[e], x_recv.at[k], plane((k // 4, k % 4)))

    send_points(0, (1, 2, 3), range(1, 8))
    send(ys.at[0], ys.at[target_slot(0, 1)], p_send, p_recv.at[0], sibling)
    send(bown, bsib, b_sem.at[0], b_sem.at[1], sibling)
    wait(ys.at[pl.ds(0, 3)], y_send.at[0])
    send_points(1, (4, 5, 6, 7), ())
    wait(xs.at[pl.ds(0, 7)], x_send.at[0])
    send_points(1, (), range(8, 16))

    def forward(r):
        slot = target_slot(r, 0)
        wait(ys.at[slot], y_recv.at[r])
        send(ys.at[slot], ys.at[target_slot(r, 1)], p_send, p_recv.at[r], sibling)

    def build_source(k):
        x = xs[k]
        xn[pl.ds(source_row(k), 1), :] = jnp.sum(x * x, axis=0, keepdims=True)
        scaled = x * (2.0 * SCORE)
        hi = scaled.astype(BF16)
        lo = (scaled - hi.astype(F32)).astype(BF16)
        at = slice(k * B, k * B + B)
        X[0:64, at] = hi
        X[64:128, at] = ones
        X[128:192, at] = hi
        X[192:256, at] = lo

    def build_target(t):
        y = ys[t]
        row = target_row(t)
        norm = jnp.sum(y * y, axis=0, keepdims=True)
        yn[pl.ds(row, 1), :] = norm
        mass = (bsib if t % 8 >= 4 else bown)[pl.ds(lax.rem(row, 8), 1), :] * LOG2E
        ba[pl.ds(row, 1), :] = mass
        bias = mass - norm * SCORE
        gb[pl.ds(row, 1), :] = bias
        hi = bias.astype(BF16).astype(F32)
        mid = (bias - hi).astype(BF16).astype(F32)
        lo = bias - hi - mid
        at8 = lax.broadcasted_iota(jnp.int32, (D, B), 0)
        tail = jnp.where(at8 == 0, hi, jnp.where(at8 == 1, mid, jnp.where(at8 == 2, lo, 0.0)))
        both = jnp.concatenate([y, tail], axis=0).T
        top = both.astype(BF16).astype(F32)
        rest = jnp.where(left, both - top, pltpu.roll(top, D, 1))
        at = slice(t * B, t * B + B)
        Y[at, 0:128] = top.astype(BF16)
        Y[at, 128:256] = rest.astype(BF16)

    def scores(r0, rn, c0, cn, fresh):
        step = 256
        width = cn // 2

        def chunk(n, _):
            at = pl.ds(pl.multiple_of(c0 + n * width, width), width)
            Tb = T.at[r0 : r0 + rn, at]
            Mb, Sb = MS.at[0, :, at], MS.at[1, :, at]
            Xb = X.at[:, at]
            for h in range(width // step):
                half = slice(h * step, h * step + step)
                Tb[:, half] = jnp.dot(Y[r0 : r0 + rn, :], Xb[:, half], preferred_element_type=F32)
            for u in range(width // B):
                lane = slice(u * B, u * B + B)
                m = s = None
                if not fresh:
                    m, s = Mb[:, lane], Sb[:, lane]
                for q in range(rn // B):
                    rows = [Tb[q * B + r * 8 : q * B + r * 8 + 8, lane] for r in range(16)]
                    new = tree(jnp.maximum, rows)
                    if m is not None:
                        new = jnp.maximum(m, new)
                    total = tree(jnp.add, [jnp.exp2(r - new) for r in rows])
                    s = total if m is None else total + s * jnp.exp2(m - new)
                    m = new
                Mb[:, lane] = m
                Sb[:, lane] = s
            return 0

        lax.fori_loop(0, 2, chunk, 0)

    H = N // 2
    Q = N // 4
    for r in (1, 2, 3):
        forward(r)
    for k in range(1, 8):
        wait(xs.at[k], x_recv.at[k])
    wait(bsib, b_sem.at[1])
    for k in range(8):
        build_source(k)
    for t in range(4):
        build_target(t)
    scores(0, Q, 0, H, True)
    for r in range(4):
        wait(ys.at[0], p_recv.at[r])
    for t in range(4, 8):
        build_target(t)
    scores(Q, Q, 0, H, False)
    for r in (4, 5, 6, 7):
        forward(r)
    for k in range(8, 16):
        wait(xs.at[k], x_recv.at[k])
    for k in range(8, 16):
        build_source(k)
    scores(0, H, H, H, True)
    for t in range(8, 12):
        build_target(t)
    scores(H, Q, 0, N, False)
    for r in range(4, 8):
        wait(ys.at[0], p_recv.at[r])
    for t in range(12, 16):
        build_target(t)
    scores(H + Q, Q, 0, N, False)
    for k in range(NB):
        lane = slice(k * B, k * B + B)
        m, s = MS[0, :, lane], MS[1, :, lane]
        top = jnp.max(m, axis=0, keepdims=True)
        total = jnp.sum(s * jnp.exp2(m - top), axis=0, keepdims=True)
        ex1[chip, pl.ds(source_row(k), 1), :] = top + jnp.log(total) * LOG2E

    def exchange(ex, mine, targets, e):
        for o in targets:
            send(ex.at[mine], ex.at[mine], e_send.at[e], e_recv.at[e], o)
        wait(ex.at[pl.ds(0, 15)], e_recv.at[e])

    planes = [plane(o) for o in FAR]
    columns = [column(o) for o in reversed(COLUMN)]

    exchange(ex1, chip, planes, 0)
    a2 = av[pl.ds(core, NB, stride=2), :] * LOG2E
    first = a2 - lse_rows(ex1[...])
    fa[...] = first
    for n in range(NB):
        fb8[:, n * B : (n + 1) * B] = jnp.broadcast_to(fa[pl.ds(source_row(n), 1), :], (8, B))

    def half2(t, _):
        block = pl.ds(pl.multiple_of(t * B, B), B)
        Tb, mb, sb = T.at[block], mbuf.at[block], sbuf.at[block]
        for q in range(NB):
            at = slice(q * 8, q * 8 + 8)
            parts = []
            for n in range(NB):
                lane = slice(n * B, (n + 1) * B)
                value = Tb[at, lane] + fb8[:, lane]
                Tb[at, lane] = value
                parts.append(value)
            top = tree(jnp.maximum, parts)
            mb[at, :] = top
            sb[at, :] = tree(jnp.add, [jnp.exp2(p - top) for p in parts])
        return 0

    lax.fori_loop(0, NB, half2, 0)

    for t in range(NB):
        at = slice(t * B, t * B + B)
        m = mbuf[at, :].T
        s = sbuf[at, :].T
        top = jnp.max(m, axis=0, keepdims=True)
        total = jnp.sum(s * jnp.exp2(m - top), axis=0, keepdims=True)
        ex2[here, pl.ds(target_row(t), 1), :] = top + jnp.log(total) * LOG2E

    exchange(ex2, here, columns, 1)
    b2 = ba[...]
    total2 = lse_rows(ex2[...])
    gb[...] = gb[...] - total2 + b2
    fa[...] = b2 - total2

    R8[...] = jnp.zeros((8, N), F32)

    for t in range(NB):
        mbuf[t * B : t * B + B, :] = jnp.broadcast_to(fa[pl.ds(target_row(t), 1), :], (B, B)).T

    def lanes_of(my):
        return pl.ds(pl.multiple_of(lax.rem(yi + 4 - my, 4) * Q, Q), Q)

    for e in range(2):
        spans = [lanes_of(2 * e), lanes_of(2 * e + 1)]

        def half3(t, _):
            block = pl.ds(pl.multiple_of(t * B, B), B)
            mb = mbuf.at[block]
            for span in spans:
                Tb, Rb = T.at[block, span], R8.at[:, span]
                for h in range(2):
                    ats = [slice((h * 8 + q) * 8, (h * 8 + q) * 8 + 8) for q in range(8)]
                    shifts = [mb[at, :] for at in ats]
                    for n in range(4):
                        lane = slice(n * B, (n + 1) * B)
                        values = []
                        for at, shift in zip(ats, shifts):
                            value = jnp.exp2(Tb[at, lane] + shift)
                            Tb[at, lane] = value
                            values.append(value)
                        Rb[:, lane] = Rb[:, lane] + tree(jnp.add, values)
            return 0

        lax.fori_loop(0, NB, half3, 0)
        for g, span in enumerate(spans):
            Rb = R8.at[:, span]
            for n in range(4):
                row = (2 * e + g) * 4 + lax.rem(xi + 4 - n, 4)
                ex3[chip, pl.ds(row, 1), :] = jnp.sum(Rb[:, n * B : (n + 1) * B], axis=0, keepdims=True)
        part = ex3.at[chip, pl.ds(8 * e, 8)]
        for o in planes:
            send(part, part, r_send.at[e], r_recv.at[e], o)

    for e in range(2):
        wait(ex3.at[pl.ds(0, 15), pl.ds(0, 8)], r_recv.at[e])
        rows = slice(8 * e, 8 * e + 8)
        total3 = jnp.sum(ex3[:, rows, :], axis=0)
        fsib[0, rows, :] = xn[rows, :] + (first[rows] - jnp.log(total3) * LOG2E) * UNIT
        fa[rows, :] = jnp.exp2(a2[rows]) / total3
        spans = [lanes_of(2 * e), lanes_of(2 * e + 1)]
        for g, span in enumerate(spans):
            vb = v8.at[:, span]
            for n in range(4):
                row = (2 * e + g) * 4 + lax.rem(xi + 4 - n, 4)
                vb[:, n * B : (n + 1) * B] = jnp.broadcast_to(fa[pl.ds(row, 1), :], (8, B))
        if e == 1:
            send(fsib.at[0], fsib.at[1], f_sem.at[0], f_sem.at[1], sibling)

        def half4(t, _):
            block = pl.ds(pl.multiple_of(t * B, B), B)
            sb = sbuf.at[block]
            for h in range(2):
                ats = [slice((h * 8 + q) * 8, (h * 8 + q) * 8 + 8) for q in range(8)]
                sums = [sb[at, :] for at in ats] if e else [None] * 8
                for span in spans:
                    Tb, vb = T.at[block, span], v8.at[:, span]
                    for n in range(4):
                        lane = slice(n * B, (n + 1) * B)
                        weight = vb[:, lane]
                        for q, at in enumerate(ats):
                            value = Tb[at, lane] * weight
                            sums[q] = value if sums[q] is None else sums[q] + value
                for q, at in enumerate(ats):
                    sb[at, :] = sums[q]
            return 0

        lax.fori_loop(0, NB, half4, 0)

    for t in range(NB):
        total = jnp.sum(sbuf[t * B : t * B + B, :].T, axis=0, keepdims=True)
        ex4[here, pl.ds(target_row(t), 1), :] = total

    exchange(ex4, here, columns, 3)
    total4 = jnp.sum(ex4[...], axis=0)
    fa[...] = yn[...] + (gb[...] - jnp.log(total4) * LOG2E) * UNIT
    g_ref[...] = fa[pl.ds(pl.multiple_of(core * 8, 8), 8), :]
    wait(fsib.at[1], f_sem.at[1])
    f_ref[pl.ds(core, NB, stride=2), :] = fsib[0]
    f_ref[pl.ds(1 - core, NB, stride=2), :] = fsib[1]

    wait(xs.at[pl.ds(0, 8)], x_send.at[1])
    wait(ys.at[pl.ds(0, 4)], y_send.at[1])
    wait(ys.at[pl.ds(0, 8)], p_send)
    wait(bown, b_sem.at[0])
    wait(fsib.at[0], f_sem.at[0])
    for e in range(2):
        wait(ex3.at[pl.ds(0, 15), pl.ds(0, 8)], r_send.at[e])
    for e, ex in ((0, ex1), (1, ex2), (3, ex4)):
        wait(ex.at[pl.ds(0, 15)], e_send.at[e])


def on_device(src_points, tgt_points, src_logmass, tgt_logmass):
    vmem = pl.BlockSpec(memory_space=pltpu.VMEM)
    dma = pltpu.SemaphoreType.DMA
    exchange = pltpu.VMEM((NB, NB, B), F32)
    f, g = pl.pallas_call(
        kernel,
        out_shape=(jax.ShapeDtypeStruct((32, B), F32), jax.ShapeDtypeStruct((8, B), F32)),
        in_specs=[pl.BlockSpec(memory_space=pl.ANY)] * 4,
        out_specs=(vmem, vmem),
        scratch_shapes=[
            pltpu.VMEM((NB, D, B), F32),
            pltpu.VMEM((NB, D, B), F32),
            pltpu.VMEM((32, B), F32),
            pltpu.VMEM((8, B), F32),
            pltpu.VMEM((8, B), F32),
            pltpu.VMEM((256, N), BF16),
            pltpu.VMEM((N, 256), BF16),
            pltpu.VMEM((N, N), F32),
            pltpu.VMEM((2, 8, N), F32),
            pltpu.VMEM((NB, B), F32),
            pltpu.VMEM((NB, B), F32),
            pltpu.VMEM((NB, B), F32),
            pltpu.VMEM((NB, B), F32),
            pltpu.VMEM((NB, B), F32),
            pltpu.VMEM((8, N), F32),
            pltpu.VMEM((N, B), F32),
            pltpu.VMEM((N, B), F32),
            pltpu.VMEM((8, N), F32),
            pltpu.VMEM((8, N), F32),
            exchange, exchange, exchange, exchange,
            pltpu.VMEM((2, NB, B), F32),
            dma((4,)), dma((2,)), dma((16,)), dma((2,)), dma((8,)), dma, dma((8,)), dma((2,)), dma((4,)), dma((4,)), dma((2,)), dma((2,)), dma((2,)),
        ],
        compiler_params=pltpu.CompilerParams(
            collective_id=0, has_side_effects=True, vmem_limit_bytes=56 << 20
        ),
    )(src_points, tgt_points, src_logmass.reshape(32, B), tgt_logmass.reshape(8, B))
    return f.reshape(-1), g.reshape(-1)


def solution(mesh):
    return jax.shard_map(
        on_device,
        mesh=mesh,
        in_specs=(P(None, ("row", "col")), P(None, ("col", "row")), P("row"), P("col")),
        out_specs=(P("row"), P("col")),
        check_vma=False,
    )
```
